128 devices in a mesh: aa: 4 (over z_hi, core), ba: 32 (over y, z_lo, x).
Axes of the slice: x: 4, y: 4, z: 4 (z_hi: 2, z_lo: 2; z = z_hi * 2 + z_lo), core: 2. Of those that a mesh axis runs over, the one named last changes fastest.
Arguments:
- source_feats: bfloat16 [4, 10, 1024], P('aa'), may hold values from -4 to 4
- target_feats: bfloat16 [256, 512, 1024], P('ba'), may hold values from -4 to 4
- first_kernel: bfloat16 [16, 1, 3, 3, 3, 3], replicated, may hold values from -0.625 to 0.625
- first_bias: float32 [16], replicated, may hold values from -3 to 3
- second_kernel: bfloat16 [1, 16, 3, 3, 3, 3], replicated, may hold values from -0.15625 to 0.15625
- second_bias: float32 [1], replicated, may hold values from -1 to 1
Outputs:
- matches: float32 [4, 10, 256, 512], P('aa', None, 'ba')
The draws below stay inside these ranges and needn't reach their ends.
All inputs are finite; a program needn't handle non-finite values.
Results may differ from the reference program's by a relative error of at most 0.0059.
Values may be sent and summed in bfloat16 or wider, within the bound.
No kernel may reach another device: no remote copies, remote signals or barrier semaphores. Data moves between devices by JAX's collectives and lax.ppermute only.
A program may use at most 192 MiB of HBM per device.

```python
import jax
import jax.numpy as jnp
from jax import lax

C = 1024
HID = 16
AW = 10
BR_DEV = 8
BW = 512
AR = 4
BH = 256


def source_base(key):
    source_key = jax.random.fold_in(key, 101)
    values = jax.random.normal(source_key, (AR * AW, C), jnp.float32)
    return jnp.clip(values, -4.0, 4.0)


def draw_source_feats(key, part):
    return source_base(key).reshape(AR, AW, C).astype(jnp.bfloat16)


def draw_target_feats(key, part):
    target_key = jax.random.fold_in(key, 102)
    values = jax.random.normal(target_key, (BH * BW, C), jnp.float32)
    planted_ids = jax.random.permutation(jax.random.fold_in(key, 103), BH * BW)[:AR * AW]
    values = values.at[planted_ids].add(0.2 * source_base(key))
    return jnp.clip(values, -4.0, 4.0).reshape(BH, BW, C).astype(jnp.bfloat16)


def gaussian(own_key, shape, width, reach, kind=jnp.bfloat16):
    return jnp.clip(width * jax.random.normal(own_key, shape, jnp.float32), -reach, reach).astype(kind)


def setup_inputs(seed: int = 0) -> dict:
    seeds = jax.random.split(jax.random.key(seed), 7)
    source_feats = draw_source_feats(jax.random.fold_in(seeds[6], 71), 0)
    target_feats = draw_target_feats(jax.random.fold_in(seeds[6], 71), 0)
    first_kernel = gaussian(seeds[2], (HID, 1, 3, 3, 3, 3), 81 ** -0.5, 0.625)
    first_bias = gaussian(seeds[3], (HID,), 0.5, 3.0, jnp.float32)
    second_kernel = gaussian(seeds[4], (1, HID, 3, 3, 3, 3), (HID * 81) ** -0.5, 0.15625)
    second_bias = jnp.clip(jax.random.uniform(seeds[5], (1,), jnp.float32, -1.0, 1.0), -1.0, 1.0)
    return dict(source_feats=source_feats, target_feats=target_feats, first_kernel=first_kernel, first_bias=first_bias, second_kernel=second_kernel, second_bias=second_bias)


eps = 1e-5


def stencil(volume, kernel, offset):
    rows_a = volume.shape[0] - 2
    cols_a = volume.shape[1] - 2
    chan_in = volume.shape[2]
    rows_b = volume.shape[3] - 2
    cols_b = volume.shape[4] - 2
    chan_out = kernel.shape[0]
    running_sum = jnp.zeros((rows_a * cols_a, chan_out, rows_b, cols_b), jnp.float32)
    for shift_a in range(3):
        stacked = jnp.concatenate([volume[shift_a:shift_a + rows_a, shift_c:shift_c + cols_a] for shift_c in range(3)], axis=2)
        stacked = stacked.reshape(rows_a * cols_a, 3 * chan_in, rows_b + 2, cols_b + 2)
        taps = jnp.transpose(kernel[:, :, shift_a], (0, 2, 1, 3, 4)).reshape(chan_out, 3 * chan_in, 3, 3)
        running_sum = running_sum + lax.conv_general_dilated(stacked, taps, (1, 1), "VALID", dimension_numbers=("NCHW", "OIHW", "NCHW"), precision=lax.Precision.HIGHEST, preferred_element_type=jnp.float32)
    return running_sum.reshape(rows_a, cols_a, chan_out, rows_b, cols_b) + offset[None, None, :, None, None]


def pad_sides(volume):
    return jnp.pad(volume, ((0, 0), (1, 1), (0, 0), (0, 0), (1, 1)))


def reference(source_feats, target_feats, first_kernel, first_bias, second_kernel, second_bias):
    flat_source = source_feats.reshape(AR * AW, C).astype(jnp.float32)
    flat_target = target_feats.reshape(BH * BW, C).astype(jnp.float32)
    product = jnp.dot(flat_source, flat_target.T, precision=lax.Precision.HIGHEST)
    correlation = (product * (C ** -0.5)).astype(jnp.bfloat16)
    correlation = lax.optimization_barrier(correlation).astype(jnp.float32)
    correlation = correlation.reshape(AR, AW, 1, BH, BW)
    padded = jnp.pad(correlation, ((2, 2), (1, 1), (0, 0), (2, 2), (1, 1)))
    kernel_one = first_kernel.astype(jnp.float32)
    kernel_two = second_kernel.astype(jnp.float32)
    blocks = BH // BR_DEV
    zero_index = jnp.zeros((), jnp.int32)

    def one_block(block_index):
        source_row = block_index // blocks
        b_start = (block_index % blocks) * BR_DEV
        window = lax.dynamic_slice(padded, (source_row, zero_index, zero_index, b_start, zero_index), (5, AW + 2, 1, BR_DEV + 4, BW + 2))
        pre = stencil(window, kernel_one, first_bias)
        row_ids = source_row - 1 + jnp.arange(3, dtype=jnp.int32)
        target_ids = b_start - 1 + jnp.arange(BR_DEV + 2, dtype=jnp.int32)
        keep_rows = ((row_ids >= 0) & (row_ids < AR)).astype(jnp.float32)
        keep_target = ((target_ids >= 0) & (target_ids < BH)).astype(jnp.float32)
        hidden = (jnp.maximum(pre, 0.0) * keep_rows[:, None, None, None, None] * keep_target[None, None, None, :, None]).astype(jnp.bfloat16)
        hidden = lax.optimization_barrier(hidden).astype(jnp.float32)
        logits = stencil(pad_sides(hidden), kernel_two, second_bias)
        return jax.nn.softplus(logits[0, :, 0])

    scores = lax.map(one_block, jnp.arange(AR * blocks, dtype=jnp.int32))
    scores = scores.reshape(AR, blocks, AW, BR_DEV, BW).transpose(0, 2, 1, 3, 4).reshape(AR, AW, BH, BW)
    best_source = jnp.max(scores, axis=(2, 3))
    best_target = jnp.max(scores, axis=(0, 1))
    return scores * (scores / (best_target[None, None] + eps)) * (scores / (best_source[:, :, None, None] + eps))
```

```python
import functools

import jax
import jax.numpy as jnp
import numpy as np
from jax import lax
from jax.experimental import pallas as pl
from jax.experimental.pallas import tpu as pltpu
from jax.sharding import PartitionSpec as P

C = 1024
HID = 16
AW = 10
AR = 4
CELLS = AR * AW
PAD = 48
BW = 512
BR = 8
TAPS = 9
K1 = TAPS * PAD
M1 = CELLS * HID
M2 = TAPS * CELLS
M2P = 368
EPS = 1e-5
BF = jnp.bfloat16
F32 = jnp.float32
VMEM_LIMIT = 56 * 1024 * 1024


def softplus(v):
    return jnp.maximum(v, 0.0) + jnp.log1p(jnp.exp(-jnp.abs(v)))


def shifted(x, t):
    if t == 1:
        return x
    lane = lax.broadcasted_iota(jnp.int32, x.shape, 1)
    if t == 0:
        return jnp.where(lane == 0, 0.0, pltpu.roll(x, 1, 1))
    return jnp.where(lane == BW - 1, 0.0, pltpu.roll(x, BW - 1, 1))


def column_tables():
    table = np.full((8, 640), -1000, np.int32)
    col = np.arange(K1)
    cell = col % PAD
    table[0, :K1] = np.where(cell < CELLS, cell // AW, -1000)
    table[1, :K1] = np.where(cell < CELLS, cell % AW, 0)
    table[2, :K1] = col // PAD
    table[3, :K1] = np.where((col // PAD == 4) & (cell >= CELLS), cell - CELLS, -1000)
    col = np.arange(M1)
    table[4] = col // HID
    table[5] = col % HID
    return table


def prep_kernel(table_ref, k1_ref, b1_ref, k2_ref, w1_ref, w2_ref, w2f_ref):
    me = lax.axis_index("aa")
    rank = table_ref[0:1, :K1]
    real = rank >= 0
    rank = jnp.where(real, lax.bitwise_xor(jnp.where(real, rank, 0), me), -1000)
    cell = rank * AW + table_ref[1:2, :K1]
    tap = table_ref[2:3, :K1]
    slot = table_ref[3:4, :K1]
    weight = k1_ref[...]
    row_id = lax.broadcasted_iota(jnp.int32, (81, K1), 0)
    spread = []
    for uv in range(9):
        pick = jnp.where(row_id == uv * 9 + tap, 1.0, 0.0).astype(BF)
        spread.append(jnp.dot(weight, pick, preferred_element_type=F32))
    bias = b1_ref[...]
    hi = bias.astype(BF).astype(F32)
    mid = (bias - hi).astype(BF).astype(F32)
    low = bias - hi - mid
    slot16 = jnp.broadcast_to(slot, (HID, K1))
    base = jnp.where(
        slot16 == 0, hi, jnp.where(slot16 == 1, mid, jnp.where(slot16 == 2, low, 0.0))
    )
    cell16 = jnp.broadcast_to(cell, (HID, K1))
    for r in range(AR):
        for j in range(AW):
            block = base
            for u in range(3):
                for v in range(3):
                    if 0 <= r + u - 1 < AR and 0 <= j + v - 1 < AW:
                        where = (r + u - 1) * AW + j + v - 1
                        block = jnp.where(cell16 == where, spread[u * 3 + v], block)
            start = (r * AW + j) * HID
            w1_ref[start : start + HID, :] = block.astype(BF)
    chan = table_ref[5:6, :]
    pick = jnp.where(
        lax.broadcasted_iota(jnp.int32, (HID, M1), 0) == chan, 1.0, 0.0
    ).astype(BF)
    rows = jnp.dot(k2_ref[...], pick, preferred_element_type=F32)
    own = lax.broadcasted_iota(jnp.int32, (CELLS, M1), 0)
    own_row = jnp.where(own >= 10, 1, 0) + jnp.where(own >= 20, 1, 0) + jnp.where(own >= 30, 1, 0)
    own_col = own - own_row * AW
    own_cell = lax.bitwise_xor(own_row, me) * AW + own_col
    gap = table_ref[4:5, :] - own_cell
    gaps = [
        jnp.where(own_col >= 1, gap, 1000),
        gap,
        jnp.where(own_col <= AW - 2, gap, 1000),
    ]
    for st in range(9):
        block = jnp.zeros((CELLS, M1), F32)
        for u in range(3):
            for v in range(3):
                line = rows[(u * 3 + v) * 9 + st : (u * 3 + v) * 9 + st + 1, :]
                block = jnp.where(gaps[v] == (u - 1) * AW + v - 1, line, block)
        w2f_ref[st * CELLS : (st + 1) * CELLS, :] = block
    w2f_ref[M2:M2P, :] = jnp.zeros((M2P - M2, M1), F32)
    w2_ref[...] = w2f_ref[...].astype(BF)


def prep(k1, b1, k2):
    vm = pl.BlockSpec(memory_space=pltpu.VMEM)
    return pl.pallas_call(
        prep_kernel,
        out_shape=(
            jax.ShapeDtypeStruct((M1, K1), BF),
            jax.ShapeDtypeStruct((M2P, M1), BF),
        ),
        in_specs=[vm] * 4,
        out_specs=(vm, vm),
        scratch_shapes=[pltpu.VMEM((M2P, M1), F32)],
        compiler_params=pltpu.CompilerParams(vmem_limit_bytes=VMEM_LIMIT),
        cost_estimate=pl.CostEstimate(flops=10**9, bytes_accessed=10**6, transcendentals=0),
        name="prep",
    )(column_tables(), k1, b1, k2)


def corr_kernel(s0, s1, s2, s3, target_ref, out_ref, lo_ref, hi_ref, stage, feats):
    p = pl.program_id(0)

    @pl.when(p == 0)
    def _():
        for n, ref in enumerate((s0, s1, s2, s3)):
            stage[n * AW : (n + 1) * AW, :] = ref[0].astype(F32)
        feats[0:CELLS, :] = stage[...]
        feats[CELLS:PAD, :] = jnp.zeros((PAD - CELLS, C), F32)

    product = lax.dot_general(
        feats[...].astype(BF),
        target_ref[0],
        (((1,), (1,)), ((), ())),
        preferred_element_type=F32,
    )
    value = (product * C ** (-0.5)).astype(BF).astype(F32)
    row = lax.broadcasted_iota(jnp.int32, value.shape, 0)
    value = jnp.where(row >= CELLS, 1.0, value)
    center = value.astype(BF)
    out_ref[0:PAD, :] = shifted(value, 0).astype(BF)
    out_ref[PAD : 2 * PAD, :] = center
    out_ref[2 * PAD : 3 * PAD, :] = shifted(value, 2).astype(BF)
    for n in range(2):

        @pl.when(p == n)
        def _():
            lo_ref[:, n * BW : (n + 1) * BW] = center

        @pl.when(p == BR - 2 + n)
        def _():
            hi_ref[:, n * BW : (n + 1) * BW] = center


def correlate(sources, target):
    src = pl.BlockSpec((1, AW, C), lambda p: (0, 0, 0))
    edge = pl.BlockSpec((PAD, 2 * BW), lambda p: (0, 0))
    return pl.pallas_call(
        corr_kernel,
        grid=(BR,),
        out_shape=(
            jax.ShapeDtypeStruct((3 * PAD, BR * BW), BF),
            jax.ShapeDtypeStruct((PAD, 2 * BW), BF),
            jax.ShapeDtypeStruct((PAD, 2 * BW), BF),
        ),
        in_specs=[src] * 4 + [pl.BlockSpec((1, BW, C), lambda p: (p, 0, 0))],
        out_specs=(pl.BlockSpec((3 * PAD, BW), lambda p: (0, p)), edge, edge),
        scratch_shapes=[pltpu.VMEM((CELLS, C), F32), pltpu.VMEM((PAD, C), F32)],
        compiler_params=pltpu.CompilerParams(vmem_limit_bytes=VMEM_LIMIT),
        name="correlate",
    )(*sources, target)


def conv_kernel(
    blocks, x_ref, lo_ref, hi_ref, w1_ref, w2_ref, b2_ref, s_ref, bt_ref, mx_ref, edge, acc
):
    place = lax.axis_index("ba")
    for n, ref in enumerate((lo_ref, hi_ref)):
        for m in range(2):
            value = ref[:, m * BW : (m + 1) * BW].astype(F32)
            for t in range(3):
                edge[n * 2 + m, t * PAD : (t + 1) * PAD, :] = shifted(value, t).astype(BF)

    def ext(e):
        if e < 2:
            return edge[e]
        if e >= BR + 2:
            return edge[e - BR]
        return x_ref[:, (e - 2) * BW : (e - 1) * BW]

    for h in range(BR + 2):
        x = jnp.concatenate([ext(h), ext(h + 1), ext(h + 2)], axis=0)
        hidden = jnp.dot(w1_ref[...], x, preferred_element_type=F32)
        hidden = jnp.maximum(hidden, 0.0)
        if h == 0:
            hidden = jnp.where(place > 0, hidden, 0.0)
        if h == BR + 1:
            hidden = jnp.where(place < blocks - 1, hidden, 0.0)
        z = jnp.dot(w2_ref[...], hidden.astype(BF), preferred_element_type=F32)
        for s in range(3):
            p = h - s
            if 0 <= p < BR:
                part = z[s * 3 * CELLS : (s + 1) * 3 * CELLS, :]
                if s == 0:
                    acc[p] = part
                else:
                    acc[p] = acc[p] + part
    b2 = b2_ref[0]
    best = None
    for p in range(BR):
        logits = (
            acc[p, CELLS : 2 * CELLS, :]
            + shifted(acc[p, 0:CELLS, :], 0)
            + shifted(acc[p, 2 * CELLS : 3 * CELLS, :], 2)
            + b2
        )
        bt_ref[p : p + 1, :] = softplus(jnp.max(logits, axis=0, keepdims=True))
        mine = logits[0:AW, :]
        best = mine if best is None else jnp.maximum(best, mine)
        score = softplus(mine)
        for j in range(AW):
            s_ref[j, p : p + 1, :] = score[j : j + 1, :]
    top = jnp.max(best, axis=1, keepdims=True)
    row = lax.broadcasted_iota(jnp.int32, (AW, 128), 0)
    lane = lax.broadcasted_iota(jnp.int32, (AW, 128), 1)
    line = jnp.sum(jnp.where(row == lane, top, 0.0), axis=0, keepdims=True)
    mx_ref[...] = jnp.broadcast_to(line, mx_ref.shape)


def convolve(blocks, x, lo, hi, w1, w2, b2):
    vm = pl.BlockSpec(memory_space=pltpu.VMEM)
    return pl.pallas_call(
        functools.partial(conv_kernel, blocks),
        out_shape=(
            jax.ShapeDtypeStruct((AW, BR, BW), F32),
            jax.ShapeDtypeStruct((BR, BW), F32),
            jax.ShapeDtypeStruct((blocks, 128), F32),
        ),
        in_specs=[vm] * 5 + [pl.BlockSpec(memory_space=pltpu.SMEM)],
        out_specs=(vm, vm, vm),
        scratch_shapes=[
            pltpu.VMEM((4, 3 * PAD, BW), BF),
            pltpu.VMEM((BR, 3 * CELLS, BW), F32),
        ],
        compiler_params=pltpu.CompilerParams(vmem_limit_bytes=VMEM_LIMIT),
        name="convolve",
    )(x, lo, hi, w1, w2, b2)


def final_kernel(s_ref, bt_ref, mx_ref, out_ref):
    top = softplus(jnp.max(mx_ref[...], axis=0, keepdims=True))
    best = bt_ref[...] + EPS
    for j in range(AW):
        s = s_ref[j]
        out_ref[0, j] = s * (s / best) * (s / (top[:, j : j + 1] + EPS))


def finish(s, bt, mx):
    vm = pl.BlockSpec(memory_space=pltpu.VMEM)
    return pl.pallas_call(
        final_kernel,
        out_shape=jax.ShapeDtypeStruct((1, AW, BR, BW), F32),
        in_specs=[vm] * 3,
        out_specs=vm,
        name="finish",
    )(s, bt, mx)


def per_device(source, target, first_kernel, first_bias, second_kernel, second_bias):
    blocks = lax.axis_size("ba")
    size = lax.axis_size("aa")
    sources = [source] + [
        lax.ppermute(source, "aa", [(i, i ^ k) for i in range(size)]) for k in range(1, size)
    ]
    w1, w2 = prep(
        first_kernel.reshape(HID, 81), first_bias[:, None], second_kernel.reshape(HID, 81).T
    )
    x, lo, hi = correlate(sources, target)
    up = [(i, i + 1) for i in range(blocks - 1)]
    before = lax.ppermute(hi, "ba", up)
    after = lax.ppermute(lo, "ba", [(j, i) for i, j in up])
    s, bt, mx = convolve(blocks, x, before, after, w1, w2, second_bias)
    mx = lax.all_to_all(mx, "ba", 0, 0, tiled=True)
    return finish(s, bt, mx)


def solution(mesh):
    return jax.shard_map(
        per_device,
        mesh=mesh,
        in_specs=(P("aa", None, None), P("ba", None, None), P(), P(), P(), P()),
        out_specs=P("aa", None, "ba", None),
        check_vma=False,
    )
```

```python
import functools

import jax
import jax.numpy as jnp
import numpy as np
from jax import lax
from jax.experimental import pallas as pl
from jax.experimental.pallas import tpu as pltpu
from jax.sharding import PartitionSpec as P

C = 1024
HID = 16
AW = 10
AR = 4
CELLS = AR * AW
PAD = 48
BW = 512
BR = 8
TAPS = 9
K1 = TAPS * PAD
M1 = CELLS * HID
M2 = TAPS * CELLS
M2P = 368
EPS = 1e-5
BF = jnp.bfloat16
F32 = jnp.float32
VMEM_LIMIT = 20 * 1024 * 1024


def cost(us):
    return pl.CostEstimate(flops=int(us * 1e9), bytes_accessed=int(us * 3e6), transcendentals=0)


def softplus(v):
    return jnp.maximum(v, 0.0) + jnp.log1p(jnp.exp(-jnp.abs(v)))


def shifted(x, t):
    if t == 1:
        return x
    lane = lax.broadcasted_iota(jnp.int32, x.shape, 1)
    if t == 0:
        return jnp.where(lane == 0, 0.0, pltpu.roll(x, 1, 1))
    return jnp.where(lane == BW - 1, 0.0, pltpu.roll(x, BW - 1, 1))


def column_tables():
    table = np.full((8, 640), -1000, np.int32)
    col = np.arange(K1)
    cell = col % PAD
    table[0, :K1] = np.where(cell < CELLS, cell // AW, -1000)
    table[1, :K1] = np.where(cell < CELLS, cell % AW, 0)
    table[2, :K1] = col // PAD
    table[3, :K1] = np.where((col // PAD == 4) & (cell >= CELLS), cell - CELLS, -1000)
    col = np.arange(M1)
    table[4] = col // HID
    table[5] = col % HID
    return table


def prep_kernel(table_ref, k1_ref, b1_ref, k2_ref, w1_ref, w2_ref, w2f_ref, flat_ref):
    me = lax.axis_index("aa")

    def lines(ref):
        for n in range(27):
            u, v, w = n // 9, n // 3 % 3, n % 3
            flat_ref[3 * n : 3 * n + 3, :] = ref[u, v, w].astype(F32)
        return flat_ref[...].astype(BF)

    rank = table_ref[0:1, :K1]
    real = rank >= 0
    rank = jnp.where(real, lax.bitwise_xor(jnp.where(real, rank, 0), me), -1000)
    cell = rank * AW + table_ref[1:2, :K1]
    tap = table_ref[2:3, :K1]
    slot = table_ref[3:4, :K1]
    weight = lines(k1_ref)
    row_id = lax.broadcasted_iota(jnp.int32, (81, K1), 0)
    spread = []
    for uv in range(9):
        pick = jnp.where(row_id == uv * 9 + tap, 1.0, 0.0).astype(BF)
        spread.append(
            lax.dot_general(
                weight, pick, (((0,), (0,)), ((), ())), preferred_element_type=F32
            )
        )
    square = (HID, HID)
    on = lax.broadcasted_iota(jnp.int32, square, 0) == lax.broadcasted_iota(jnp.int32, square, 1)
    bias = jnp.sum(jnp.where(on, b1_ref[...], 0.0), axis=1, keepdims=True)
    hi = bias.astype(BF).astype(F32)
    mid = (bias - hi).astype(BF).astype(F32)
    low = bias - hi - mid
    slot16 = jnp.broadcast_to(slot, (HID, K1))
    base = jnp.where(
        slot16 == 0, hi, jnp.where(slot16 == 1, mid, jnp.where(slot16 == 2, low, 0.0))
    )
    cell16 = jnp.broadcast_to(cell, (HID, K1))
    for r in range(AR):
        for j in range(AW):
            block = base
            for u in range(3):
                for v in range(3):
                    if 0 <= r + u - 1 < AR and 0 <= j + v - 1 < AW:
                        where = (r + u - 1) * AW + j + v - 1
                        block = jnp.where(cell16 == where, spread[u * 3 + v], block)
            start = (r * AW + j) * HID
            w1_ref[start : start + HID, :] = block.astype(BF)
    chan = table_ref[5:6, :]
    pick = jnp.where(
        lax.broadcasted_iota(jnp.int32, (HID, M1), 0) == chan, 1.0, 0.0
    ).astype(BF)
    rows = jnp.dot(lines(k2_ref), pick, preferred_element_type=F32)
    own = lax.broadcasted_iota(jnp.int32, (CELLS, M1), 0)
    own_row = jnp.where(own >= 10, 1, 0) + jnp.where(own >= 20, 1, 0) + jnp.where(own >= 30, 1, 0)
    own_col = own - own_row * AW
    own_cell = lax.bitwise_xor(own_row, me) * AW + own_col
    gap = table_ref[4:5, :] - own_cell
    gaps = [
        jnp.where(own_col >= 1, gap, 1000),
        gap,
        jnp.where(own_col <= AW - 2, gap, 1000),
    ]
    for st in range(9):
        block = jnp.zeros((CELLS, M1), F32)
        for u in range(3):
            for v in range(3):
                line = rows[(u * 3 + v) * 9 + st : (u * 3 + v) * 9 + st + 1, :]
                block = jnp.where(gaps[v] == (u - 1) * AW + v - 1, line, block)
        w2f_ref[st * CELLS : (st + 1) * CELLS, :] = block
    w2f_ref[M2:M2P, :] = jnp.zeros((M2P - M2, M1), F32)
    w2_ref[...] = w2f_ref[...].astype(BF)


def prep(k1, b1, k2):
    vm = pl.BlockSpec(memory_space=pltpu.VMEM)
    return pl.pallas_call(
        prep_kernel,
        out_shape=(
            jax.ShapeDtypeStruct((M1, K1), BF),
            jax.ShapeDtypeStruct((M2P, M1), BF),
        ),
        in_specs=[vm] * 4,
        out_specs=(vm, vm),
        scratch_shapes=[pltpu.VMEM((M2P, M1), F32), pltpu.VMEM((81, HID), F32)],
        compiler_params=pltpu.CompilerParams(vmem_limit_bytes=VMEM_LIMIT),
        cost_estimate=cost(3.0),
        name="prep",
    )(column_tables(), k1, b1, k2)


def correlation(feats, block):
    product = lax.dot_general(
        feats, block, (((1,), (1,)), ((), ())), preferred_element_type=F32
    )
    value = (product * C ** (-0.5)).astype(BF).astype(F32)
    row = lax.broadcasted_iota(jnp.int32, value.shape, 0)
    return jnp.where(row >= CELLS, 1.0, value)


def edge_kernel(s0, s1, s2, s3, target_ref, w1_ref, feats_ref, lo_ref, hi_ref, stage):
    for n, ref in enumerate((s0, s1, s2, s3)):
        stage[n * AW : (n + 1) * AW, :] = ref[0].astype(F32)
    stage[CELLS:PAD, :] = jnp.zeros((PAD - CELLS, C), F32)
    feats = stage[...].astype(BF)
    feats_ref[...] = feats
    for ref, first in ((lo_ref, 0), (hi_ref, BR - 2)):
        for n in range(2):
            ref[:, n * BW : (n + 1) * BW] = correlation(feats, target_ref[first + n]).astype(BF)


def edges(sources, target, w1):
    vm = pl.BlockSpec(memory_space=pltpu.VMEM)
    edge = jax.ShapeDtypeStruct((PAD, 2 * BW), BF)
    return pl.pallas_call(
        edge_kernel,
        out_shape=(jax.ShapeDtypeStruct((PAD, C), BF), edge, edge),
        in_specs=[vm] * 5 + [pl.BlockSpec(memory_space=pl.ANY)],
        out_specs=(vm, vm, vm),
        scratch_shapes=[pltpu.VMEM((PAD, C), F32)],
        compiler_params=pltpu.CompilerParams(vmem_limit_bytes=VMEM_LIMIT),
        cost_estimate=cost(2.0),
        name="edges",
    )(*sources, target, w1)


def three_shifts(value):
    return jnp.concatenate([shifted(value, t).astype(BF) for t in range(3)], axis=0)


def hidden_row(w1, parts):
    x = jnp.concatenate(parts, axis=0)
    return jnp.maximum(jnp.dot(w1, x, preferred_element_type=F32), 0.0)


def spread_row(h, z, acc, seen, keep):
    for s in range(3):
        p = h - s
        if 0 <= p < BR:
            part = z[s * 3 * CELLS : (s + 1) * 3 * CELLS, :]
            at = keep(p)
            if p in seen:
                acc[at] = acc[at] + part
            else:
                acc[at] = part
                seen.add(p)


def logit_row(sums, b2):
    return (
        sums[CELLS : 2 * CELLS, :]
        + shifted(sums[0:CELLS, :], 0)
        + shifted(sums[2 * CELLS : 3 * CELLS, :], 2)
        + b2
    )


def emit_row(n, logits, s_ref, bt_ref, best):
    bt_ref[n : n + 1, :] = softplus(jnp.max(logits, axis=0, keepdims=True))
    mine = logits[0:AW, :]
    score = softplus(mine)
    for j in range(AW):
        s_ref[j, n : n + 1, :] = score[j : j + 1, :]
    return mine if best is None else jnp.maximum(best, mine)


INNER = (2, 3, 4, 5)
OUTER = (0, 1, 6, 7)


def inner_kernel(
    feats_ref, target_ref, lo_ref, hi_ref, w1_ref, w2_ref, b2_ref,
    s_ref, bt_ref, best_ref, sums_ref, x, acc,
):
    feats = feats_ref[...]
    for n in range(2):
        x[n] = three_shifts(lo_ref[:, n * BW : (n + 1) * BW].astype(F32))
        x[BR - 2 + n] = three_shifts(hi_ref[:, n * BW : (n + 1) * BW].astype(F32))
    for p in range(2, BR - 2):
        x[p] = three_shifts(correlation(feats, target_ref[p]))
    seen = set()
    for h in range(2, BR):
        hidden = hidden_row(w1_ref[...], [x[h - 2], x[h - 1], x[h]])
        z = jnp.dot(w2_ref[...], hidden.astype(BF), preferred_element_type=F32)
        spread_row(h, z, acc, seen, lambda p: p)
    best = None
    for n, p in enumerate(INNER):
        best = emit_row(n, logit_row(acc[p], b2_ref[0]), s_ref, bt_ref, best)
    best_ref[...] = best
    for n, p in enumerate(OUTER):
        sums_ref[n] = acc[p]


def inner(feats, target, lo, hi, w1, w2, b2):
    vm = pl.BlockSpec(memory_space=pltpu.VMEM)
    return pl.pallas_call(
        inner_kernel,
        out_shape=(
            jax.ShapeDtypeStruct((AW, 4, BW), F32),
            jax.ShapeDtypeStruct((4, BW), F32),
            jax.ShapeDtypeStruct((AW, BW), F32),
            jax.ShapeDtypeStruct((4, 3 * CELLS, BW), F32),
        ),
        in_specs=[vm] * 6 + [pl.BlockSpec(memory_space=pltpu.SMEM)],
        out_specs=(vm, vm, vm, vm),
        scratch_shapes=[
            pltpu.VMEM((BR, 3 * PAD, BW), BF),
            pltpu.VMEM((BR, 3 * CELLS, BW), F32),
        ],
        compiler_params=pltpu.CompilerParams(vmem_limit_bytes=VMEM_LIMIT),
        cost_estimate=cost(8.0),
        name="inner",
    )(feats, target, lo, hi, w1, w2, b2)


def outer_kernel(
    blocks, lo_ref, hi_ref, before_ref, after_ref, w1_ref, w2_ref, b2_ref, sums_ref, best_ref,
    s_ref, bt_ref, mx_ref, acc,
):
    place = lax.axis_index("ba")
    first, last = place == 0, place == blocks - 1

    def row(ref, n, drop=None):
        value = ref[:, n * BW : (n + 1) * BW].astype(F32)
        if drop is not None:
            value = jnp.where(drop, 0.0, value)
        return three_shifts(value)

    near = [row(before_ref, 0, first), row(before_ref, 1, first), row(lo_ref, 0), row(lo_ref, 1)]
    far = [row(hi_ref, 0), row(hi_ref, 1), row(after_ref, 0, last), row(after_ref, 1, last)]
    for n in range(4):
        acc[n] = sums_ref[n]
    seen = set(OUTER)
    for h, parts, drop in (
        (0, near[0:3], first),
        (1, near[1:4], None),
        (BR, far[0:3], None),
        (BR + 1, far[1:4], last),
    ):
        hidden = hidden_row(w1_ref[...], parts)
        if drop is not None:
            hidden = jnp.where(drop, 0.0, hidden)
        z = jnp.dot(w2_ref[...], hidden.astype(BF), preferred_element_type=F32)
        spread_row(h, z, acc, seen, OUTER.index)
    best = best_ref[...]
    for n in range(4):
        best = emit_row(n, logit_row(acc[n], b2_ref[0]), s_ref, bt_ref, best)
    top = jnp.max(best, axis=1, keepdims=True)
    row_id = lax.broadcasted_iota(jnp.int32, (AW, 128), 0)
    lane = lax.broadcasted_iota(jnp.int32, (AW, 128), 1)
    line = jnp.sum(jnp.where(row_id == lane, top, 0.0), axis=0, keepdims=True)
    mx_ref[...] = jnp.broadcast_to(line, mx_ref.shape)


def outer(blocks, lo, hi, before, after, w1, w2, b2, sums, best):
    vm = pl.BlockSpec(memory_space=pltpu.VMEM)
    return pl.pallas_call(
        functools.partial(outer_kernel, blocks),
        out_shape=(
            jax.ShapeDtypeStruct((AW, 4, BW), F32),
            jax.ShapeDtypeStruct((4, BW), F32),
            jax.ShapeDtypeStruct((blocks, 128), F32),
        ),
        in_specs=[vm] * 6 + [pl.BlockSpec(memory_space=pltpu.SMEM)] + [vm] * 2,
        out_specs=(vm, vm, vm),
        scratch_shapes=[pltpu.VMEM((4, 3 * CELLS, BW), F32)],
        compiler_params=pltpu.CompilerParams(vmem_limit_bytes=VMEM_LIMIT),
        cost_estimate=cost(4.0),
        name="outer",
    )(lo, hi, before, after, w1, w2, b2, sums, best)


def final_kernel(s1_ref, bt1_ref, s2_ref, bt2_ref, mx_ref, out_ref):
    top = softplus(jnp.max(mx_ref[...], axis=0, keepdims=True))
    best1 = bt1_ref[...] + EPS
    best2 = bt2_ref[...] + EPS
    for j in range(AW):
        cell = top[:, j : j + 1] + EPS
        s = s1_ref[j]
        out_ref[0, j, 2:6, :] = s * (s / best1) * (s / cell)
        s = s2_ref[j]
        both = s * (s / best2) * (s / cell)
        out_ref[0, j, 0:2, :] = both[0:2]
        out_ref[0, j, 6:8, :] = both[2:4]


def finish(s1, bt1, s2, bt2, mx):
    vm = pl.BlockSpec(memory_space=pltpu.VMEM)
    return pl.pallas_call(
        final_kernel,
        out_shape=jax.ShapeDtypeStruct((1, AW, BR, BW), F32),
        in_specs=[vm] * 5,
        out_specs=vm,
        compiler_params=pltpu.CompilerParams(vmem_limit_bytes=4 * 1024 * 1024),
        name="finish",
    )(s1, bt1, s2, bt2, mx)


def per_device(source, target, first_kernel, first_bias, second_kernel, second_bias):
    blocks = lax.axis_size("ba")
    size = lax.axis_size("aa")
    sources = [source] + [
        lax.ppermute(source, "aa", [(i, i ^ k) for i in range(size)]) for k in range(1, size)
    ]
    w1, w2 = prep(
        jnp.transpose(first_kernel[:, 0], (1, 2, 3, 4, 0)),
        first_bias[None, :],
        jnp.transpose(second_kernel[0], (1, 2, 3, 4, 0)),
    )
    feats, lo, hi = edges(sources, target, w1)
    up = [(i, (i + 1) % blocks) for i in range(blocks)]
    before = lax.ppermute(hi, "ba", up)
    after = lax.ppermute(lo, "ba", [(j, i) for i, j in up])
    s1, bt1, best, sums = inner(feats, target, lo, hi, w1, w2, second_bias)
    s2, bt2, mx = outer(blocks, lo, hi, before, after, w1, w2, second_bias, sums, best)
    mx = lax.all_to_all(mx, "ba", 0, 0, tiled=True)
    return finish(s1, bt1, s2, bt2, mx)


def solution(mesh):
    return jax.shard_map(
        per_device,
        mesh=mesh,
        in_specs=(P("aa", None, None), P("ba", None, None), P(), P(), P(), P()),
        out_specs=P("aa", None, "ba", None),
        check_vma=False,
    )
```

```python
import functools

import jax
import jax.numpy as jnp
from jax import lax
from jax.experimental import pallas as pl
from jax.experimental.pallas import tpu as pltpu
from jax.sharding import PartitionSpec as P

C = 1024
HID = 16
AW = 10
AR = 4
CELLS = AR * AW
PAD = 48
BW = 512
BR = 8
TAPS = 9
K1 = TAPS * PAD
M1 = CELLS * HID
NEAR = 3 * AW * HID
HALF = 24
GROUP = 2 * HALF
M2 = TAPS * GROUP
M3 = 224
EPS = 1e-5
BF = jnp.bfloat16
F32 = jnp.float32
VMEM_LIMIT = 20 * 1024 * 1024


def cost(us):
    return pl.CostEstimate(flops=int(us * 1e9), bytes_accessed=int(us * 3e6), transcendentals=0)


def softplus(v):
    return jnp.maximum(v, 0.0) + jnp.log1p(jnp.exp(-jnp.abs(v)))


def shifted(x, t):
    if t == 1:
        return x
    lane = lax.broadcasted_iota(jnp.int32, x.shape, 1)
    if t == 0:
        return jnp.where(lane == 0, 0.0, pltpu.roll(x, 1, 1))
    return jnp.where(lane == BW - 1, 0.0, pltpu.roll(x, BW - 1, 1))


def rank_of(me, slot):
    return (
        me,
        lax.bitwise_xor(me, 1),
        jnp.where(me < 2, 2, 1),
        jnp.where(me < 2, 3, 0),
    )[slot]


def prep_kernel(
    k1_ref, b1_ref, k2_ref, w1_ref, far1_ref, w2_ref, far2_ref, w2f_ref, far2f_ref, flat_ref
):
    me = lax.axis_index("aa")

    def lines(ref):
        for n in range(27):
            u, v, w = n // 9, n // 3 % 3, n % 3
            flat_ref[3 * n : 3 * n + 3, :] = ref[u, v, w].astype(F32)
        return flat_ref[...].astype(BF)

    col = lax.broadcasted_iota(jnp.int32, (1, K1), 1)
    tap = lax.shift_right_logical(col * 1366, 16)
    place = col - tap * PAD
    rank = lax.shift_right_logical(place * 6554, 16)
    cell = lax.bitwise_xor(rank, me) * AW + place - rank * AW
    cell = jnp.where(place < CELLS, cell, -1000)
    slot = jnp.where((tap == 4) & (place >= CELLS), place - CELLS, -1000)
    weight = lines(k1_ref)
    row_id = lax.broadcasted_iota(jnp.int32, (81, K1), 0)
    spread = []
    for uv in range(9):
        pick = jnp.where(row_id == uv * 9 + tap, 1.0, 0.0).astype(BF)
        spread.append(
            lax.dot_general(weight, pick, (((0,), (0,)), ((), ())), preferred_element_type=F32)
        )
    square = (HID, HID)
    on = lax.broadcasted_iota(jnp.int32, square, 0) == lax.broadcasted_iota(jnp.int32, square, 1)
    bias = jnp.sum(jnp.where(on, b1_ref[...], 0.0), axis=1, keepdims=True)
    hi = bias.astype(BF).astype(F32)
    mid = (bias - hi).astype(BF).astype(F32)
    low = bias - hi - mid
    slot16 = jnp.broadcast_to(slot, (HID, K1))
    base = jnp.where(
        slot16 == 0, hi, jnp.where(slot16 == 1, mid, jnp.where(slot16 == 2, low, 0.0))
    )
    cell16 = jnp.broadcast_to(cell, (HID, K1))
    for r in range(AR):
        away = cell16 - rank_of(me, r) * AW
        for j in range(AW):
            block = base
            for u in range(3):
                for v in range(3):
                    if 0 <= j + v - 1 < AW:
                        where = (u - 1) * AW + j + v - 1
                        block = jnp.where(away == where, spread[u * 3 + v], block)
            start = (r * AW + j) * HID
            if start < NEAR:
                w1_ref[start : start + HID, :] = block.astype(BF)
            else:
                far1_ref[start - NEAR : start - NEAR + HID, :] = block.astype(BF)
    col = lax.broadcasted_iota(jnp.int32, (1, M1), 1)
    chan = lax.bitwise_and(col, HID - 1)
    place = lax.shift_right_logical(col, 4)
    slot = lax.shift_right_logical(place * 6554, 16)
    rank = jnp.where(
        slot == 0,
        rank_of(me, 0),
        jnp.where(slot == 1, rank_of(me, 1), jnp.where(slot == 2, rank_of(me, 2), rank_of(me, 3))),
    )
    cell = rank * AW + place - slot * AW
    pick = jnp.where(lax.broadcasted_iota(jnp.int32, (HID, M1), 0) == chan, 1.0, 0.0).astype(BF)
    rows = jnp.dot(lines(k2_ref), pick, preferred_element_type=F32)
    for first in (0, 2):
        line_id = lax.broadcasted_iota(jnp.int32, (HALF, M1), 0)
        upper = line_id >= AW
        own_col = line_id - jnp.where(upper, AW, 0)
        own = jnp.where(upper, rank_of(me, first + 1), rank_of(me, first)) * AW + own_col
        gap = jnp.where(line_id < 2 * AW, cell - own, 1000)
        gaps = [
            jnp.where(own_col >= 1, gap, 1000),
            gap,
            jnp.where(own_col <= AW - 2, gap, 1000),
        ]
        for st in range(9):
            block = jnp.zeros((HALF, M1), F32)
            for u in range(3):
                for v in range(3):
                    n = (u * 3 + v) * 9 + st
                    block = jnp.where(gaps[v] == (u - 1) * AW + v - 1, rows[n : n + 1, :], block)
            start = st * GROUP + first // 2 * HALF
            w2f_ref[start : start + HALF, :] = block
            if first == 2:
                far2f_ref[st * HALF : (st + 1) * HALF, :] = block[:, NEAR:M1]
    far2f_ref[TAPS * HALF : M3, :] = jnp.zeros((M3 - TAPS * HALF, M1 - NEAR), F32)
    w2_ref[...] = w2f_ref[:, :NEAR].astype(BF)
    far2_ref[...] = far2f_ref[...].astype(BF)


def prep(k1, b1, k2):
    vm = pl.BlockSpec(memory_space=pltpu.VMEM)
    return pl.pallas_call(
        prep_kernel,
        out_shape=(
            jax.ShapeDtypeStruct((NEAR, K1), BF),
            jax.ShapeDtypeStruct((M1 - NEAR, K1), BF),
            jax.ShapeDtypeStruct((M2, NEAR), BF),
            jax.ShapeDtypeStruct((M3, M1 - NEAR), BF),
        ),
        in_specs=[vm] * 3,
        out_specs=(vm,) * 4,
        scratch_shapes=[
            pltpu.VMEM((M2, M1), F32),
            pltpu.VMEM((M3, M1 - NEAR), F32),
            pltpu.VMEM((81, HID), F32),
        ],
        compiler_params=pltpu.CompilerParams(vmem_limit_bytes=VMEM_LIMIT),
        cost_estimate=cost(3.0),
        name="prep",
    )(k1, b1, k2)


def correlation(feats, block):
    product = lax.dot_general(
        feats, block, (((1,), (1,)), ((), ())), preferred_element_type=F32
    )
    value = (product * C ** (-0.5)).astype(BF).astype(F32)
    row = lax.broadcasted_iota(jnp.int32, value.shape, 0)
    return jnp.where(row >= CELLS, 1.0, value)


def edge_kernel(s0, s1, s2, s3, target_ref, w1_ref, feats_ref, lo_ref, hi_ref, stage):
    for n, ref in enumerate((s0, s1, s2, s3)):
        stage[n * AW : (n + 1) * AW, :] = ref[0].astype(F32)
    stage[CELLS:PAD, :] = jnp.zeros((PAD - CELLS, C), F32)
    feats = stage[...].astype(BF)
    feats_ref[...] = feats
    for ref, first in ((lo_ref, 0), (hi_ref, BR - 2)):
        for n in range(2):
            ref[:, n * BW : (n + 1) * BW] = correlation(feats, target_ref[first + n]).astype(BF)


def edges(sources, target, w1):
    vm = pl.BlockSpec(memory_space=pltpu.VMEM)
    edge = jax.ShapeDtypeStruct((PAD, 2 * BW), BF)
    return pl.pallas_call(
        edge_kernel,
        out_shape=(jax.ShapeDtypeStruct((PAD, C), BF), edge, edge),
        in_specs=[vm] * 5 + [pl.BlockSpec(memory_space=pl.ANY)],
        out_specs=(vm, vm, vm),
        scratch_shapes=[pltpu.VMEM((PAD, C), F32)],
        compiler_params=pltpu.CompilerParams(vmem_limit_bytes=VMEM_LIMIT),
        cost_estimate=cost(2.0),
        name="edges",
    )(*sources, target, w1)


def three_shifts(value):
    return jnp.concatenate([shifted(value, t).astype(BF) for t in range(3)], axis=0)


def hidden_row(w1, parts, drop=None):
    x = jnp.concatenate(parts, axis=0)
    value = jnp.maximum(jnp.dot(w1, x, preferred_element_type=F32), 0.0)
    if drop is not None:
        value = jnp.where(drop, 0.0, value)
    return value.astype(BF)


def spread_row(h, group, w2, hidden, acc, seen, at):
    z = jnp.dot(w2, hidden, preferred_element_type=F32)
    for s in range(3):
        p = h - s
        if 0 <= p < BR:
            part = z[s * 3 * group : (s + 1) * 3 * group, :]
            if p in seen:
                acc[at(p)] = acc[at(p)] + part
            else:
                acc[at(p)] = part
                seen.add(p)


def logit_row(sums, b2):
    return sums[1] + shifted(sums[0], 0) + shifted(sums[2], 2) + b2


def halves(acc, n, half):
    starts = [t * GROUP + half * HALF for t in range(3)]
    return [acc[n, start : start + HALF, :] for start in starts]


def emit_row(n, logits, s_ref, top_ref, best):
    top_ref[n : n + 1, :] = jnp.max(logits[0 : 2 * AW, :], axis=0, keepdims=True)
    mine = logits[0:AW, :]
    score = softplus(mine)
    for j in range(AW):
        s_ref[j, n : n + 1, :] = score[j : j + 1, :]
    return mine if best is None else jnp.maximum(best, mine)


def keep_far(acc, n, far_ref):
    for t, part in enumerate(halves(acc, n[0], 1)):
        far_ref[n[1], t * HALF : (t + 1) * HALF, :] = part


INNER = (2, 3, 4, 5)
OUTER = (0, 1, 6, 7)


def inner_kernel(
    feats_ref, target_ref, lo_ref, hi_ref, w1_ref, w2_ref, b2_ref,
    s_ref, top_ref, best_ref, sums_ref, x, far_ref, acc,
):
    feats = feats_ref[...]
    for n in range(2):
        x[n] = three_shifts(lo_ref[:, n * BW : (n + 1) * BW].astype(F32))
        x[BR - 2 + n] = three_shifts(hi_ref[:, n * BW : (n + 1) * BW].astype(F32))
    for p in INNER:
        x[p] = three_shifts(correlation(feats, target_ref[p]))
    seen = set()
    for h in range(2, BR):
        hidden = hidden_row(w1_ref[...], [x[h - 2], x[h - 1], x[h]])
        spread_row(h, GROUP, w2_ref[...], hidden, acc, seen, lambda p: p)
    best = None
    for n, p in enumerate(INNER):
        best = emit_row(n, logit_row(halves(acc, p, 0), b2_ref[0]), s_ref, top_ref, best)
        keep_far(acc, (p, n), far_ref)
    best_ref[...] = best
    for n, p in enumerate(OUTER):
        sums_ref[n] = acc[p]


def inner(feats, target, lo, hi, w1, w2, b2):
    vm = pl.BlockSpec(memory_space=pltpu.VMEM)
    return pl.pallas_call(
        inner_kernel,
        out_shape=(
            jax.ShapeDtypeStruct((AW, 4, BW), F32),
            jax.ShapeDtypeStruct((4, BW), F32),
            jax.ShapeDtypeStruct((AW, BW), F32),
            jax.ShapeDtypeStruct((4, 3 * GROUP, BW), F32),
            jax.ShapeDtypeStruct((BR, 3 * PAD, BW), BF),
            jax.ShapeDtypeStruct((4, 3 * HALF, BW), F32),
        ),
        in_specs=[vm] * 6 + [pl.BlockSpec(memory_space=pltpu.SMEM)],
        out_specs=(vm,) * 6,
        scratch_shapes=[pltpu.VMEM((BR, 3 * GROUP, BW), F32)],
        compiler_params=pltpu.CompilerParams(vmem_limit_bytes=VMEM_LIMIT),
        cost_estimate=cost(3.0),
        name="inner",
    )(feats, target, lo, hi, w1, w2, b2)


def halo_rows(ref, drop):
    cuts = [ref[:, n * BW : (n + 1) * BW] for n in range(2)]
    return [three_shifts(jnp.where(drop, 0.0, cut.astype(F32))) for cut in cuts]


def outer_kernel(
    blocks, x_ref, before_ref, after_ref, w1_ref, w2_ref, b2_ref, sums_ref, best_ref,
    s_ref, top_ref, mx_ref, far_ref, acc,
):
    place = lax.axis_index("ba")
    first, last = place == 0, place == blocks - 1
    halo = halo_rows(before_ref, first) + halo_rows(after_ref, last)
    for n in range(4):
        acc[n] = sums_ref[n]
    seen = set(OUTER)
    near = [halo[0], halo[1], x_ref[0], x_ref[1]]
    far = [x_ref[BR - 2], x_ref[BR - 1], halo[2], halo[3]]
    for h, parts, drop in (
        (0, near[0:3], first),
        (1, near[1:4], None),
        (BR, far[0:3], None),
        (BR + 1, far[1:4], last),
    ):
        hidden = hidden_row(w1_ref[...], parts, drop)
        spread_row(h, GROUP, w2_ref[...], hidden, acc, seen, OUTER.index)
    best = best_ref[...]
    for n in range(4):
        best = emit_row(n, logit_row(halves(acc, n, 0), b2_ref[0]), s_ref, top_ref, best)
        keep_far(acc, (n, n), far_ref)
    top = jnp.max(best, axis=1, keepdims=True)
    row_id = lax.broadcasted_iota(jnp.int32, (AW, 128), 0)
    lane = lax.broadcasted_iota(jnp.int32, (AW, 128), 1)
    line = jnp.sum(jnp.where(row_id == lane, top, 0.0), axis=0, keepdims=True)
    mx_ref[...] = jnp.broadcast_to(line, mx_ref.shape)


def outer(blocks, x, before, after, w1, w2, b2, sums, best):
    vm = pl.BlockSpec(memory_space=pltpu.VMEM)
    return pl.pallas_call(
        functools.partial(outer_kernel, blocks),
        out_shape=(
            jax.ShapeDtypeStruct((AW, 4, BW), F32),
            jax.ShapeDtypeStruct((4, BW), F32),
            jax.ShapeDtypeStruct((blocks, 128), F32),
            jax.ShapeDtypeStruct((4, 3 * HALF, BW), F32),
        ),
        in_specs=[vm] * 5 + [pl.BlockSpec(memory_space=pltpu.SMEM)] + [vm] * 2,
        out_specs=(vm,) * 4,
        scratch_shapes=[pltpu.VMEM((4, 3 * GROUP, BW), F32)],
        compiler_params=pltpu.CompilerParams(vmem_limit_bytes=VMEM_LIMIT),
        cost_estimate=cost(1),
        name="outer",
    )(x, before, after, w1, w2, b2, sums, best)


def rest_kernel(
    blocks, x_ref, before_ref, after_ref, far1_ref, far2_ref, w1_ref, w2_ref, b2_ref,
    s1_ref, top1_ref, s2_ref, top2_ref, s_ref, q_ref, acc, tops,
):
    place = lax.axis_index("ba")
    first, last = place == 0, place == blocks - 1
    rows = [
        *halo_rows(before_ref, first),
        *(x_ref[p] for p in range(BR)),
        *halo_rows(after_ref, last),
    ]
    for p in range(BR):
        acc[p] = far1_ref[INNER.index(p)] if p in INNER else far2_ref[OUTER.index(p)]
    seen = set(range(BR))
    for h in range(BR + 2):
        drop = first if h == 0 else last if h == BR + 1 else None
        hidden = hidden_row(w1_ref[...], rows[h : h + 3], drop)
        spread_row(h, HALF, w2_ref[...], hidden, acc, seen, lambda p: p)
    for p in range(BR):
        sums = [acc[p, t * HALF : (t + 1) * HALF, :] for t in range(3)]
        logits = logit_row(sums, b2_ref[0])
        top = jnp.max(logits[0 : 2 * AW, :], axis=0, keepdims=True)
        ref, n = (top1_ref, INNER.index(p)) if p in INNER else (top2_ref, OUTER.index(p))
        tops[p : p + 1, :] = jnp.maximum(top, ref[n : n + 1, :])
    best = softplus(tops[...]) + EPS
    for j in range(AW):
        s = jnp.concatenate([s2_ref[j, 0:2], s1_ref[j], s2_ref[j, 2:4]], axis=0)
        s_ref[j] = s
        q_ref[j] = s * (s / best)


def rest(blocks, x, before, after, far1, far2, w1, w2, b2, s1, top1, s2, top2):
    vm = pl.BlockSpec(memory_space=pltpu.VMEM)
    full = jax.ShapeDtypeStruct((AW, BR, BW), F32)
    return pl.pallas_call(
        functools.partial(rest_kernel, blocks),
        out_shape=(full, full),
        in_specs=[vm] * 7 + [pl.BlockSpec(memory_space=pltpu.SMEM)] + [vm] * 4,
        out_specs=(vm, vm),
        scratch_shapes=[pltpu.VMEM((BR, 3 * HALF, BW), F32), pltpu.VMEM((BR, BW), F32)],
        compiler_params=pltpu.CompilerParams(vmem_limit_bytes=VMEM_LIMIT),
        cost_estimate=cost(1),
        name="rest",
    )(x, before, after, far1, far2, w1, w2, b2, s1, top1, s2, top2)


def final_kernel(s_ref, q_ref, mx_ref, out_ref):
    top = softplus(jnp.max(mx_ref[...], axis=0, keepdims=True))
    for j in range(AW):
        out_ref[0, j] = q_ref[j] * (s_ref[j] / (top[:, j : j + 1] + EPS))


def finish(s, q, mx):
    vm = pl.BlockSpec(memory_space=pltpu.VMEM)
    return pl.pallas_call(
        final_kernel,
        out_shape=jax.ShapeDtypeStruct((1, AW, BR, BW), F32),
        in_specs=[vm] * 3,
        out_specs=vm,
        compiler_params=pltpu.CompilerParams(vmem_limit_bytes=4 * 1024 * 1024),
        name="finish",
    )(s, q, mx)


def per_device(source, target, first_kernel, first_bias, second_kernel, second_bias):
    blocks = lax.axis_size("ba")
    size = lax.axis_size("aa")
    sources = [source] + [
        lax.ppermute(source, "aa", [(i, i ^ k) for i in range(size)]) for k in range(1, size)
    ]
    w1, w1_far, w2, w2_far = prep(
        jnp.transpose(first_kernel[:, 0], (1, 2, 3, 4, 0)),
        first_bias[None, :],
        jnp.transpose(second_kernel[0], (1, 2, 3, 4, 0)),
    )
    feats, lo, hi = edges(sources, target, w1)
    up = [(i, (i + 1) % blocks) for i in range(blocks)]
    before = lax.ppermute(hi, "ba", up)
    after = lax.ppermute(lo, "ba", [(j, i) for i, j in up])
    s1, top1, best, sums, x, far1 = inner(feats, target, lo, hi, w1, w2, second_bias)
    s2, top2, mx, far2 = outer(
        blocks, x, before, after, w1, w2, second_bias, sums, best
    )
    mx = lax.all_to_all(mx, "ba", 0, 0, tiled=True)
    s, q = rest(
        blocks, x, before, after, far1, far2, w1_far, w2_far, second_bias, s1, top1, s2, top2
    )
    return finish(s, q, mx)


def solution(mesh):
    return jax.shard_map(
        per_device,
        mesh=mesh,
        in_specs=(P("aa", None, None), P("ba", None, None), P(), P(), P(), P()),
        out_specs=P("aa", None, "ba", None),
        check_vma=False,
    )
```

```python
import functools

import jax
import jax.numpy as jnp
from jax import lax
from jax.experimental import pallas as pl
from jax.experimental.pallas import tpu as pltpu
from jax.sharding import PartitionSpec as P

C = 1024
HID = 16
AW = 10
AR = 4
CELLS = AR * AW
PAIR = 24
PAD = 2 * PAIR
BW = 512
BR = 8
LINE = 80
HALF = 3 * LINE
GAP = 16
K1 = 2 * (HALF + GAP)
ROW = AW * HID
M1 = AR * ROW
M2 = 3 * CELLS
EPS = 1e-5
BF = jnp.bfloat16
F32 = jnp.float32
VMEM_LIMIT = 20 * 1024 * 1024


def cost(us):
    return pl.CostEstimate(flops=int(us * 1e9), bytes_accessed=int(us * 3e6), transcendentals=0)


def softplus(v):
    return jnp.maximum(v, 0.0) + jnp.log1p(jnp.exp(-jnp.abs(v)))


def shifted(x, t):
    if t == 1:
        return x
    lane = lax.broadcasted_iota(jnp.int32, x.shape, 1)
    if t == 0:
        return jnp.where(lane == 0, 0.0, pltpu.roll(x, 1, 1))
    return jnp.where(lane == BW - 1, 0.0, pltpu.roll(x, BW - 1, 1))


def table_kernel(out_ref):
    col = lax.broadcasted_iota(jnp.int32, (8, K1 // 2), 1)
    s = lax.shift_right_logical(col * 820, 16)
    rest = col - s * LINE
    t = lax.shift_right_logical(rest * 2731, 16)
    place = rest - t * PAIR
    real = (s < 3) & (t < 3)
    tap = s * 3 + t
    cell = jnp.where(real & (place < 2 * AW), place, -1000)
    one = jnp.where(real & (tap == 4) & (place >= 2 * AW), place - 2 * AW, -1000)
    row = lax.broadcasted_iota(jnp.int32, (8, K1 // 2), 0)
    out_ref[...] = jnp.where(row == 0, tap, jnp.where(row == 1, cell, one))


def tables():
    return pl.pallas_call(
        table_kernel,
        out_shape=jax.ShapeDtypeStruct((8, K1 // 2), jnp.int32),
        out_specs=pl.BlockSpec(memory_space=pltpu.VMEM),
        compiler_params=pltpu.CompilerParams(vmem_limit_bytes=4 * 1024 * 1024),
        cost_estimate=cost(4.0),
        name="tables",
    )()


def prep_kernel(table_ref, k1_ref, b1_ref, k2_ref, w1_ref, w2_ref, w2f_ref, flat_ref):
    me = lax.axis_index("aa")

    def lines(ref):
        for n in range(27):
            u, v, w = n // 9, n // 3 % 3, n % 3
            flat_ref[3 * n : 3 * n + 3, :] = ref[u, v, w].astype(F32)
        return flat_ref[...].astype(BF)

    tap = table_ref[0:1, :]
    weight = lines(k1_ref)
    row_id = lax.broadcasted_iota(jnp.int32, (81, K1 // 2), 0)
    spread = []
    for uv in range(9):
        pick = jnp.where(row_id == uv * 9 + tap, 1.0, 0.0).astype(BF)
        spread.append(
            lax.dot_general(weight, pick, (((0,), (0,)), ((), ())), preferred_element_type=F32)
        )
    square = (HID, HID)
    on = lax.broadcasted_iota(jnp.int32, square, 0) == lax.broadcasted_iota(jnp.int32, square, 1)
    bias = jnp.sum(jnp.where(on, b1_ref[...], 0.0), axis=1, keepdims=True)
    hi = bias.astype(BF).astype(F32)
    mid = (bias - hi).astype(BF).astype(F32)
    low = bias - hi - mid
    one = jnp.broadcast_to(table_ref[2:3, :], (HID, K1 // 2))
    base = jnp.where(one == 0, hi, jnp.where(one == 1, mid, jnp.where(one == 2, low, 0.0)))
    cell = jnp.broadcast_to(table_ref[1:2, :], (HID, K1 // 2))
    for r in range(AR):
        for j in range(AW):
            for half in range(2):
                block = base if half == r // 3 else jnp.zeros_like(base)
                for u in range(3):
                    for v in range(3):
                        i = r + u - 1
                        if i // 2 == half and 0 <= j + v - 1 < AW:
                            where = i % 2 * AW + j + v - 1
                            block = jnp.where(cell == where, spread[u * 3 + v], block)
                start = (r * AW + j) * HID
                cut = slice(half * (K1 // 2), (half + 1) * (K1 // 2))
                w1_ref[start : start + HID, cut] = block.astype(BF)
    col = lax.broadcasted_iota(jnp.int32, (1, M1), 1)
    chan = lax.bitwise_and(col, HID - 1)
    pick = jnp.where(lax.broadcasted_iota(jnp.int32, (HID, M1), 0) == chan, 1.0, 0.0).astype(BF)
    rows = jnp.dot(lines(k2_ref), pick, preferred_element_type=F32)
    own = lax.broadcasted_iota(jnp.int32, (CELLS, M1), 0)
    own_row = jnp.where(own >= 10, 1, 0) + jnp.where(own >= 20, 1, 0) + jnp.where(own >= 30, 1, 0)
    own_col = own - own_row * AW
    own_cell = lax.bitwise_xor(own_row, me) * AW + own_col
    gap = lax.shift_right_logical(col, 4) - own_cell
    gaps = [
        jnp.where(own_col >= 1, gap, 1000),
        gap,
        jnp.where(own_col <= AW - 2, gap, 1000),
    ]
    for st in range(9):
        block = jnp.zeros((CELLS, M1), F32)
        for u in range(3):
            for v in range(3):
                n = (u * 3 + v) * 9 + st
                block = jnp.where(gaps[v] == (u - 1) * AW + v - 1, rows[n : n + 1, :], block)
        s, t = st // 3, st % 3
        w2f_ref[t * CELLS : (t + 1) * CELLS, s * M1 : (s + 1) * M1] = block
    w2_ref[...] = w2f_ref[...].astype(BF)


def prep(k1, b1, k2):
    vm = pl.BlockSpec(memory_space=pltpu.VMEM)
    return pl.pallas_call(
        prep_kernel,
        out_shape=(
            jax.ShapeDtypeStruct((M1, K1), BF),
            jax.ShapeDtypeStruct((M2, 3 * M1), BF),
        ),
        in_specs=[vm] * 4,
        out_specs=(vm, vm),
        scratch_shapes=[pltpu.VMEM((M2, 3 * M1), F32), pltpu.VMEM((81, HID), F32)],
        compiler_params=pltpu.CompilerParams(vmem_limit_bytes=VMEM_LIMIT),
        cost_estimate=cost(2.0),
        name="prep",
    )(tables(), k1, b1, k2)


def correlation(feats, block):
    product = lax.dot_general(
        feats, block, (((1,), (1,)), ((), ())), preferred_element_type=F32
    )
    value = (product * C ** (-0.5)).astype(BF).astype(F32)
    row = lax.broadcasted_iota(jnp.int32, value.shape, 0)
    filler = (row >= PAD - 4) | ((row >= PAIR - 4) & (row < PAIR))
    return jnp.where(filler, 1.0, value)


def edge_kernel(s0, s1, s2, s3, target_ref, w1_ref, feats_ref, lo_ref, hi_ref, stage):
    me = lax.axis_index("aa")
    given = [ref[0].astype(F32) for ref in (s0, s1, s2, s3)]
    stage[...] = jnp.zeros_like(stage)
    for n in range(AR):
        pick = given[n ^ 3]
        for k in range(3):
            pick = jnp.where(me == k, given[n ^ k], pick)
        start = n // 2 * PAIR + n % 2 * AW
        stage[start : start + AW, :] = pick
    feats = stage[...].astype(BF)
    feats_ref[...] = feats
    for ref, first in ((lo_ref, 0), (hi_ref, BR - 2)):
        for n in range(2):
            ref[:, n * BW : (n + 1) * BW] = correlation(feats, target_ref[first + n]).astype(BF)


def edges(sources, target, w1):
    vm = pl.BlockSpec(memory_space=pltpu.VMEM)
    edge = jax.ShapeDtypeStruct((PAD, 2 * BW), BF)
    return pl.pallas_call(
        edge_kernel,
        out_shape=(jax.ShapeDtypeStruct((PAD, C), BF), edge, edge),
        in_specs=[vm] * 5 + [pl.BlockSpec(memory_space=pl.ANY)],
        out_specs=(vm, vm, vm),
        scratch_shapes=[pltpu.VMEM((PAD, C), F32)],
        compiler_params=pltpu.CompilerParams(vmem_limit_bytes=VMEM_LIMIT),
        cost_estimate=cost(2.0),
        name="edges",
    )(*sources, target, w1)


def three_shifts(value):
    moved = [shifted(value, t) for t in range(3)]
    fill = jnp.zeros((LINE - 3 * PAIR, BW), F32)
    return jnp.concatenate(
        [
            piece
            for n in range(2)
            for piece in (*(m[n * PAIR : (n + 1) * PAIR] for m in moved), fill)
        ],
        axis=0,
    ).astype(BF)


def hidden_row(w1_ref, parts, out_ref, start, drop=None):
    low = jnp.concatenate([part[0:LINE] for part in parts], axis=0)
    high = jnp.concatenate([part[LINE : 2 * LINE] for part in parts], axis=0)
    both = jnp.concatenate([low, jnp.zeros((GAP, BW), BF), high], axis=0)
    for first, rows, begin, x in (
        (0, ROW, 0, low),
        (ROW, 2 * ROW, 0, both),
        (3 * ROW, ROW, HALF + GAP, high),
    ):
        w1 = w1_ref[first : first + rows, begin : begin + x.shape[0]]
        value = jnp.maximum(jnp.dot(w1, x, preferred_element_type=F32), 0.0)
        if drop is not None:
            value = jnp.where(drop, 0.0, value)
        out_ref[start + first : start + first + rows, :] = value.astype(BF)


def sums_of(w2_ref, hidden_ref, s, first, count):
    return jnp.dot(
        w2_ref[:, s * M1 : (s + count) * M1],
        hidden_ref[first * M1 : (first + count) * M1, :],
        preferred_element_type=F32,
    )


def logit_row(sums, b2):
    return (
        sums[CELLS : 2 * CELLS, :]
        + shifted(sums[0:CELLS, :], 0)
        + shifted(sums[2 * CELLS : 3 * CELLS, :], 2)
        + b2
    )


def emit_row(n, logits, s_ref, bt_ref, best):
    bt_ref[n : n + 1, :] = softplus(jnp.max(logits, axis=0, keepdims=True))
    mine = logits[0:AW, :]
    score = softplus(mine)
    for j in range(AW):
        s_ref[j, n : n + 1, :] = score[j : j + 1, :]
    return mine if best is None else jnp.maximum(best, mine)


def inner_kernel(
    feats_ref, target_ref, lo_ref, hi_ref, w1_ref, w2_ref, b2_ref,
    s_ref, bt_ref, best_ref, sums_ref, x, hidden,
):
    feats = feats_ref[...]
    for n in range(2):
        x[n] = three_shifts(lo_ref[:, n * BW : (n + 1) * BW].astype(F32))
        x[BR - 2 + n] = three_shifts(hi_ref[:, n * BW : (n + 1) * BW].astype(F32))
    for p in range(2, BR - 2):
        x[p] = three_shifts(correlation(feats, target_ref[p]))
    best = None
    for h in range(BR - 2):
        hidden_row(w1_ref, [x[h], x[h + 1], x[h + 2]], hidden, h * M1)
        if h >= 2:
            logits = logit_row(sums_of(w2_ref, hidden, 0, h - 2, 3), b2_ref[0])
            best = emit_row(h - 2, logits, s_ref, bt_ref, best)
    best_ref[...] = best
    sums_ref[0] = sums_of(w2_ref, hidden, 2, 0, 1)
    sums_ref[1] = sums_of(w2_ref, hidden, 1, 0, 2)
    sums_ref[2] = sums_of(w2_ref, hidden, 0, 4, 2)
    sums_ref[3] = sums_of(w2_ref, hidden, 0, 5, 1)


def inner(feats, target, lo, hi, w1, w2, b2):
    vm = pl.BlockSpec(memory_space=pltpu.VMEM)
    return pl.pallas_call(
        inner_kernel,
        out_shape=(
            jax.ShapeDtypeStruct((AW, 4, BW), F32),
            jax.ShapeDtypeStruct((4, BW), F32),
            jax.ShapeDtypeStruct((AW, BW), F32),
            jax.ShapeDtypeStruct((4, 3 * CELLS, BW), F32),
        ),
        in_specs=[vm] * 6 + [pl.BlockSpec(memory_space=pltpu.SMEM)],
        out_specs=(vm, vm, vm, vm),
        scratch_shapes=[
            pltpu.VMEM((BR, 2 * LINE, BW), BF),
            pltpu.VMEM(((BR - 2) * M1, BW), BF),
        ],
        compiler_params=pltpu.CompilerParams(vmem_limit_bytes=VMEM_LIMIT),
        cost_estimate=cost(8.0),
        name="inner",
    )(feats, target, lo, hi, w1, w2, b2)


def outer_kernel(
    blocks, lo_ref, hi_ref, before_ref, after_ref, w1_ref, w2_ref, b2_ref, sums_ref, best_ref,
    s_ref, bt_ref, mx_ref, hidden,
):
    place = lax.axis_index("ba")
    first, last = place == 0, place == blocks - 1

    def row(ref, n, drop=None):
        value = ref[:, n * BW : (n + 1) * BW].astype(F32)
        if drop is not None:
            value = jnp.where(drop, 0.0, value)
        return three_shifts(value)

    near = [row(before_ref, 0, first), row(before_ref, 1, first), row(lo_ref, 0), row(lo_ref, 1)]
    far = [row(hi_ref, 0), row(hi_ref, 1), row(after_ref, 0, last), row(after_ref, 1, last)]
    hidden_row(w1_ref, near[0:3], hidden, 0, first)
    hidden_row(w1_ref, near[1:4], hidden, M1)
    hidden_row(w1_ref, far[0:3], hidden, 2 * M1)
    hidden_row(w1_ref, far[1:4], hidden, 3 * M1, last)
    best = best_ref[...]
    for n, (s, begin, count) in enumerate(((0, 0, 2), (0, 1, 1), (2, 2, 1), (1, 2, 2))):
        sums = sums_ref[n] + sums_of(w2_ref, hidden, s, begin, count)
        best = emit_row(n, logit_row(sums, b2_ref[0]), s_ref, bt_ref, best)
    top = jnp.max(best, axis=1, keepdims=True)
    row_id = lax.broadcasted_iota(jnp.int32, (AW, 128), 0)
    lane = lax.broadcasted_iota(jnp.int32, (AW, 128), 1)
    line = jnp.sum(jnp.where(row_id == lane, top, 0.0), axis=0, keepdims=True)
    mx_ref[...] = jnp.broadcast_to(line, mx_ref.shape)


def outer(blocks, lo, hi, before, after, w1, w2, b2, sums, best):
    vm = pl.BlockSpec(memory_space=pltpu.VMEM)
    return pl.pallas_call(
        functools.partial(outer_kernel, blocks),
        out_shape=(
            jax.ShapeDtypeStruct((AW, 4, BW), F32),
            jax.ShapeDtypeStruct((4, BW), F32),
            jax.ShapeDtypeStruct((blocks, 128), F32),
        ),
        in_specs=[vm] * 6 + [pl.BlockSpec(memory_space=pltpu.SMEM)] + [vm] * 2,
        out_specs=(vm, vm, vm),
        scratch_shapes=[pltpu.VMEM((4 * M1, BW), BF)],
        compiler_params=pltpu.CompilerParams(vmem_limit_bytes=VMEM_LIMIT),
        cost_estimate=cost(4.0),
        name="outer",
    )(lo, hi, before, after, w1, w2, b2, sums, best)


def final_kernel(s1_ref, bt1_ref, s2_ref, bt2_ref, mx_ref, out_ref):
    top = softplus(jnp.max(mx_ref[...], axis=0, keepdims=True))
    best1 = bt1_ref[...] + EPS
    best2 = bt2_ref[...] + EPS
    for j in range(AW):
        cell = top[:, j : j + 1] + EPS
        s = s1_ref[j]
        out_ref[0, j, 2:6, :] = s * (s / best1) * (s / cell)
        s = s2_ref[j]
        both = s * (s / best2) * (s / cell)
        out_ref[0, j, 0:2, :] = both[0:2]
        out_ref[0, j, 6:8, :] = both[2:4]


def finish(s1, bt1, s2, bt2, mx):
    vm = pl.BlockSpec(memory_space=pltpu.VMEM)
    return pl.pallas_call(
        final_kernel,
        out_shape=jax.ShapeDtypeStruct((1, AW, BR, BW), F32),
        in_specs=[vm] * 5,
        out_specs=vm,
        compiler_params=pltpu.CompilerParams(vmem_limit_bytes=4 * 1024 * 1024),
        name="finish",
    )(s1, bt1, s2, bt2, mx)


def per_device(source, target, first_kernel, first_bias, second_kernel, second_bias):
    blocks = lax.axis_size("ba")
    size = lax.axis_size("aa")
    sources = [source] + [
        lax.ppermute(source, "aa", [(i, i ^ k) for i in range(size)]) for k in range(1, size)
    ]
    w1, w2 = prep(
        jnp.transpose(first_kernel[:, 0], (1, 2, 3, 4, 0)),
        first_bias[None, :],
        jnp.transpose(second_kernel[0], (1, 2, 3, 4, 0)),
    )
    feats, lo, hi = edges(sources, target, w1)
    up = [(i, (i + 1) % blocks) for i in range(blocks)]
    before = lax.ppermute(hi, "ba", up)
    after = lax.ppermute(lo, "ba", [(j, i) for i, j in up])
    s1, bt1, best, sums = inner(feats, target, lo, hi, w1, w2, second_bias)
    s2, bt2, mx = outer(blocks, lo, hi, before, after, w1, w2, second_bias, sums, best)
    mx = lax.all_to_all(mx, "ba", 0, 0, tiled=True)
    return finish(s1, bt1, s2, bt2, mx)


def solution(mesh):
    return jax.shard_map(
        per_device,
        mesh=mesh,
        in_specs=(P("aa", None, None), P("ba", None, None), P(), P(), P(), P()),
        out_specs=P("aa", None, "ba", None),
        check_vma=False,
    )
```

```python
import functools

import jax
import jax.numpy as jnp
from jax import lax
from jax.experimental import pallas as pl
from jax.experimental.pallas import tpu as pltpu
from jax.sharding import PartitionSpec as P

C = 1024
HID = 16
AW = 10
AR = 4
CELLS = AR * AW
PAIR = 24
PAD = 2 * PAIR
BW = 512
BR = 8
LINE = 80
HALF = 3 * LINE
GAP = 16
K1 = 2 * (HALF + GAP)
ROW = AW * HID
OWN = BR // 2
M1 = AR * ROW
M2 = 3 * CELLS
EPS = 1e-5
BF = jnp.bfloat16
F32 = jnp.float32
VMEM_LIMIT = 20 * 1024 * 1024


def cost(us):
    return pl.CostEstimate(flops=int(us * 1e9), bytes_accessed=int(us * 3e6), transcendentals=0)


def softplus(v):
    return jnp.maximum(v, 0.0) + jnp.log1p(jnp.exp(-jnp.abs(v)))


def shifted(x, t):
    if t == 1:
        return x
    lane = lax.broadcasted_iota(jnp.int32, x.shape, 1)
    if t == 0:
        return jnp.where(lane == 0, 0.0, pltpu.roll(x, 1, 1))
    return jnp.where(lane == BW - 1, 0.0, pltpu.roll(x, BW - 1, 1))


def table_kernel(out_ref):
    col = lax.broadcasted_iota(jnp.int32, (8, K1 // 2), 1)
    s = lax.shift_right_logical(col * 820, 16)
    rest = col - s * LINE
    t = lax.shift_right_logical(rest * 2731, 16)
    place = rest - t * PAIR
    real = (s < 3) & (t < 3)
    tap = s * 3 + t
    cell = jnp.where(real & (place < 2 * AW), place, -1000)
    one = jnp.where(real & (tap == 4) & (place >= 2 * AW), place - 2 * AW, -1000)
    row = lax.broadcasted_iota(jnp.int32, (8, K1 // 2), 0)
    out_ref[...] = jnp.where(row == 0, tap, jnp.where(row == 1, cell, one))


def tables():
    return pl.pallas_call(
        table_kernel,
        out_shape=jax.ShapeDtypeStruct((8, K1 // 2), jnp.int32),
        out_specs=pl.BlockSpec(memory_space=pltpu.VMEM),
        compiler_params=pltpu.CompilerParams(vmem_limit_bytes=4 * 1024 * 1024),
        cost_estimate=cost(4.0),
        name="tables",
    )()


def prep_kernel(table_ref, k1_ref, b1_ref, k2_ref, w1_ref, w2_ref, w2f_ref, flat_ref):
    me = lax.axis_index("aa")

    def lines(ref):
        for n in range(27):
            u, v, w = n // 9, n // 3 % 3, n % 3
            w = w if w == 1 else jnp.where(lax.rem(me, 2) == 0, w, 2 - w)
            flat_ref[3 * n : 3 * n + 3, :] = ref[u, v, w].astype(F32)
        return flat_ref[...].astype(BF)

    tap = table_ref[0:1, :]
    weight = lines(k1_ref)
    row_id = lax.broadcasted_iota(jnp.int32, (81, K1 // 2), 0)
    spread = []
    for uv in range(9):
        pick = jnp.where(row_id == uv * 9 + tap, 1.0, 0.0).astype(BF)
        spread.append(
            lax.dot_general(weight, pick, (((0,), (0,)), ((), ())), preferred_element_type=F32)
        )
    square = (HID, HID)
    on = lax.broadcasted_iota(jnp.int32, square, 0) == lax.broadcasted_iota(jnp.int32, square, 1)
    bias = jnp.sum(jnp.where(on, b1_ref[...], 0.0), axis=1, keepdims=True)
    hi = bias.astype(BF).astype(F32)
    mid = (bias - hi).astype(BF).astype(F32)
    low = bias - hi - mid
    one = jnp.broadcast_to(table_ref[2:3, :], (HID, K1 // 2))
    base = jnp.where(one == 0, hi, jnp.where(one == 1, mid, jnp.where(one == 2, low, 0.0)))
    cell = jnp.broadcast_to(table_ref[1:2, :], (HID, K1 // 2))
    for r in range(AR):
        for j in range(AW):
            for half in range(2):
                block = base if half == r // 3 else jnp.zeros_like(base)
                for u in range(3):
                    for v in range(3):
                        i = r + u - 1
                        if i // 2 == half and 0 <= j + v - 1 < AW:
                            where = i % 2 * AW + j + v - 1
                            block = jnp.where(cell == where, spread[u * 3 + v], block)
                start = (r * AW + j) * HID
                cut = slice(half * (K1 // 2), (half + 1) * (K1 // 2))
                w1_ref[start : start + HID, cut] = block.astype(BF)
    col = lax.broadcasted_iota(jnp.int32, (1, M1), 1)
    chan = lax.bitwise_and(col, HID - 1)
    pick = jnp.where(lax.broadcasted_iota(jnp.int32, (HID, M1), 0) == chan, 1.0, 0.0).astype(BF)
    rows = jnp.dot(lines(k2_ref), pick, preferred_element_type=F32)
    own = lax.broadcasted_iota(jnp.int32, (CELLS, M1), 0)
    own_row = jnp.where(own >= 10, 1, 0) + jnp.where(own >= 20, 1, 0) + jnp.where(own >= 30, 1, 0)
    own_col = own - own_row * AW
    own_cell = lax.bitwise_xor(own_row, me) * AW + own_col
    gap = lax.shift_right_logical(col, 4) - own_cell
    gaps = [
        jnp.where(own_col >= 1, gap, 1000),
        gap,
        jnp.where(own_col <= AW - 2, gap, 1000),
    ]
    for st in range(9):
        block = jnp.zeros((CELLS, M1), F32)
        for u in range(3):
            for v in range(3):
                n = (u * 3 + v) * 9 + st
                block = jnp.where(gaps[v] == (u - 1) * AW + v - 1, rows[n : n + 1, :], block)
        s, t = st // 3, st % 3
        w2f_ref[t * CELLS : (t + 1) * CELLS, s * M1 : (s + 1) * M1] = block
    w2_ref[...] = w2f_ref[...].astype(BF)


def prep(k1, b1, k2):
    vm = pl.BlockSpec(memory_space=pltpu.VMEM)
    return pl.pallas_call(
        prep_kernel,
        out_shape=(
            jax.ShapeDtypeStruct((M1, K1), BF),
            jax.ShapeDtypeStruct((M2, 3 * M1), BF),
        ),
        in_specs=[vm] * 4,
        out_specs=(vm, vm),
        scratch_shapes=[pltpu.VMEM((M2, 3 * M1), F32), pltpu.VMEM((81, HID), F32)],
        compiler_params=pltpu.CompilerParams(vmem_limit_bytes=VMEM_LIMIT),
        cost_estimate=cost(2.0),
        name="prep",
    )(tables(), k1, b1, k2)


def correlation(feats, block):
    product = lax.dot_general(
        feats, block, (((1,), (1,)), ((), ())), preferred_element_type=F32
    )
    value = (product * C ** (-0.5)).astype(BF).astype(F32)
    row = lax.broadcasted_iota(jnp.int32, value.shape, 0)
    filler = (row >= PAD - 4) | ((row >= PAIR - 4) & (row < PAIR))
    return jnp.where(filler, 1.0, value)


def target_row(target_ref, n):
    return target_ref[jnp.where(lax.rem(lax.axis_index("aa"), 2) == 0, n, BR - 1 - n)]


def edge_kernel(s0, s1, s2, s3, target_ref, w1_ref, feats_ref, edge_ref, stage):
    me = lax.axis_index("aa")
    given = [ref[0].astype(F32) for ref in (s0, s1, s2, s3)]
    stage[...] = jnp.zeros_like(stage)
    for n in range(AR):
        pick = given[n ^ 3]
        for k in range(3):
            pick = jnp.where(me == k, given[n ^ k], pick)
        start = n // 2 * PAIR + n % 2 * AW
        stage[start : start + AW, :] = pick
    feats = stage[...].astype(BF)
    feats_ref[...] = feats
    for n in range(2):
        value = correlation(feats, target_row(target_ref, n))
        edge_ref[:, n * BW : (n + 1) * BW] = value.astype(BF)


def edges(sources, target, w1):
    vm = pl.BlockSpec(memory_space=pltpu.VMEM)
    return pl.pallas_call(
        edge_kernel,
        out_shape=(
            jax.ShapeDtypeStruct((PAD, C), BF),
            jax.ShapeDtypeStruct((PAD, 2 * BW), BF),
        ),
        in_specs=[vm] * 5 + [pl.BlockSpec(memory_space=pl.ANY)],
        out_specs=(vm, vm),
        scratch_shapes=[pltpu.VMEM((PAD, C), F32)],
        compiler_params=pltpu.CompilerParams(vmem_limit_bytes=VMEM_LIMIT),
        cost_estimate=cost(2.0),
        name="edges",
    )(*sources, target, w1)


def three_shifts(value):
    moved = [shifted(value, t) for t in range(3)]
    fill = jnp.zeros((LINE - 3 * PAIR, BW), F32)
    return jnp.concatenate(
        [
            piece
            for n in range(2)
            for piece in (*(m[n * PAIR : (n + 1) * PAIR] for m in moved), fill)
        ],
        axis=0,
    ).astype(BF)


def hidden_row(w1_ref, parts, out_ref, start, drop=None):
    low = jnp.concatenate([part[0:LINE] for part in parts], axis=0)
    high = jnp.concatenate([part[LINE : 2 * LINE] for part in parts], axis=0)
    both = jnp.concatenate([low, jnp.zeros((GAP, BW), BF), high], axis=0)
    for first, rows, begin, x in (
        (0, ROW, 0, low),
        (ROW, 2 * ROW, 0, both),
        (3 * ROW, ROW, HALF + GAP, high),
    ):
        w1 = w1_ref[first : first + rows, begin : begin + x.shape[0]]
        value = jnp.maximum(jnp.dot(w1, x, preferred_element_type=F32), 0.0)
        if drop is not None:
            value = jnp.where(drop, 0.0, value)
        out_ref[start + first : start + first + rows, :] = value.astype(BF)


def sums_of(w2_ref, hidden_ref, s, first, count):
    return jnp.dot(
        w2_ref[:, s * M1 : (s + count) * M1],
        hidden_ref[first * M1 : (first + count) * M1, :],
        preferred_element_type=F32,
    )


def logit_row(sums, b2):
    return (
        sums[CELLS : 2 * CELLS, :]
        + shifted(sums[0:CELLS, :], 0)
        + shifted(sums[2 * CELLS : 3 * CELLS, :], 2)
        + b2
    )


def emit_row(logits, out_ref, n, best):
    mine = logits[0 : 2 * AW, :]
    out_ref[n, 0 : 2 * AW, :] = softplus(mine)
    top = jnp.max(logits, axis=0, keepdims=True)
    out_ref[n, 2 * AW : 2 * AW + 1, :] = softplus(top)
    return mine if best is None else jnp.maximum(best, mine)


def inner_kernel(
    feats_ref, target_ref, edge_ref, w1_ref, w2_ref, b2_ref,
    ready_ref, best_ref, sums_ref, near_ref, x, hidden,
):
    feats = feats_ref[...]
    for n in range(2):
        near_ref[n] = three_shifts(edge_ref[:, n * BW : (n + 1) * BW].astype(F32))
    for n in range(2, OWN + 2):
        x[n - 2] = three_shifts(correlation(feats, target_row(target_ref, n)))
    rows = [near_ref[0], near_ref[1], *(x[n] for n in range(OWN))]
    best = None
    for h in range(OWN):
        hidden_row(w1_ref, rows[h : h + 3], hidden, h * M1)
        if h >= 2:
            logits = logit_row(sums_of(w2_ref, hidden, 0, h - 2, 3), b2_ref[0])
            best = emit_row(logits, ready_ref, h - 2, best)
    best_ref[...] = best
    sums_ref[0] = sums_of(w2_ref, hidden, 2, 0, 1)
    sums_ref[1] = sums_of(w2_ref, hidden, 1, 0, 2)


def inner(feats, target, edge, w1, w2, b2):
    vm = pl.BlockSpec(memory_space=pltpu.VMEM)
    return pl.pallas_call(
        inner_kernel,
        out_shape=(
            jax.ShapeDtypeStruct((2, PAIR, BW), F32),
            jax.ShapeDtypeStruct((2 * AW, BW), F32),
            jax.ShapeDtypeStruct((2, M2, BW), F32),
            jax.ShapeDtypeStruct((2, 2 * LINE, BW), BF),
        ),
        in_specs=[vm] * 5 + [pl.BlockSpec(memory_space=pltpu.SMEM)],
        out_specs=(vm,) * 4,
        scratch_shapes=[
            pltpu.VMEM((OWN, 2 * LINE, BW), BF),
            pltpu.VMEM((OWN * M1, BW), BF),
        ],
        compiler_params=pltpu.CompilerParams(vmem_limit_bytes=VMEM_LIMIT),
        cost_estimate=cost(8.0),
        name="inner",
    )(feats, target, edge, w1, w2, b2)


def outer_kernel(
    blocks, near_ref, halo_ref, w1_ref, w2_ref, b2_ref, sums_ref, best_ref, inner_ref,
    out_ref, mx_ref, hidden,
):
    core = lax.rem(lax.axis_index("aa"), 2)
    outside = lax.axis_index("ba") == jnp.where(core == 0, 0, blocks - 1)
    rows = [
        three_shifts(jnp.where(outside, 0.0, halo_ref[:, n * BW : (n + 1) * BW].astype(F32)))
        for n in (1, 0)
    ] + [near_ref[0], near_ref[1]]
    hidden_row(w1_ref, rows[0:3], hidden, 0, outside)
    hidden_row(w1_ref, rows[1:4], hidden, M1)
    best = best_ref[...]
    for n in range(2):
        sums = sums_ref[n] + sums_of(w2_ref, hidden, 0, n, 2 - n)
        best = emit_row(logit_row(sums, b2_ref[0]), out_ref, n, best)
    out_ref[2:OWN] = inner_ref[...]
    top = jnp.max(best, axis=1, keepdims=True)
    row_id = lax.broadcasted_iota(jnp.int32, (2 * AW, 128), 0)
    lane = lax.broadcasted_iota(jnp.int32, (2 * AW, 128), 1)
    lines = [
        jnp.sum(jnp.where(row_id - n * AW == lane, top, 0.0), axis=0, keepdims=True)
        for n in range(2)
    ]
    lane = lane[0:1]
    lines = [jnp.where(lane < AW, line, 0.0) for line in lines]
    for n in range(2):
        line = jnp.where(core == n, lines[0], lines[1])
        mx_ref[n * blocks : (n + 1) * blocks, :] = jnp.broadcast_to(line, (blocks, 128))


def outer(blocks, near, halo, w1, w2, b2, sums, best, ready):
    vm = pl.BlockSpec(memory_space=pltpu.VMEM)
    return pl.pallas_call(
        functools.partial(outer_kernel, blocks),
        out_shape=(
            jax.ShapeDtypeStruct((OWN, PAIR, BW), F32),
            jax.ShapeDtypeStruct((2 * blocks, 128), F32),
        ),
        in_specs=[vm] * 4 + [pl.BlockSpec(memory_space=pltpu.SMEM)] + [vm] * 3,
        out_specs=(vm, vm),
        scratch_shapes=[pltpu.VMEM((2 * M1, BW), BF)],
        compiler_params=pltpu.CompilerParams(vmem_limit_bytes=VMEM_LIMIT),
        cost_estimate=cost(4.0),
        name="outer",
    )(near, halo, w1, w2, b2, sums, best, ready)


def final_kernel(own_ref, other_ref, mx_ref, out_ref):
    upper = lax.rem(lax.axis_index("aa"), 2) == 0
    top = softplus(jnp.max(mx_ref[...], axis=0, keepdims=True))
    row_id = lax.broadcasted_iota(jnp.int32, (AW, 128), 0)
    lane = lax.broadcasted_iota(jnp.int32, (AW, 128), 1)
    cell = jnp.sum(jnp.where(row_id == lane, top, 0.0), axis=1, keepdims=True) + EPS
    for p in range(BR):
        n = min(p, BR - 1 - p)
        here = upper if p < OWN else jnp.logical_not(upper)
        s = jnp.where(here, own_ref[n, 0:AW, :], other_ref[n, AW : 2 * AW, :])
        best = 2 * AW, 2 * AW + 1
        best = jnp.where(
            here, own_ref[n, best[0] : best[1], :], other_ref[n, best[0] : best[1], :]
        )
        value = s * (s / (best + EPS)) * (s / cell)
        for j in range(AW):
            out_ref[0, j, p : p + 1, :] = value[j : j + 1, :]


def finish(own, other, mx):
    vm = pl.BlockSpec(memory_space=pltpu.VMEM)
    return pl.pallas_call(
        final_kernel,
        out_shape=jax.ShapeDtypeStruct((1, AW, BR, BW), F32),
        in_specs=[vm] * 3,
        out_specs=vm,
        compiler_params=pltpu.CompilerParams(vmem_limit_bytes=4 * 1024 * 1024),
        name="finish",
    )(own, other, mx)


def per_device(source, target, first_kernel, first_bias, second_kernel, second_bias):
    blocks = lax.axis_size("ba")
    size = lax.axis_size("aa")
    sources = [source] + [
        lax.ppermute(source, "aa", [(i, i ^ k) for i in range(size)]) for k in range(1, size)
    ]
    w1, w2 = prep(
        jnp.transpose(first_kernel[:, 0], (1, 2, 3, 4, 0)),
        first_bias[None, :],
        jnp.transpose(second_kernel[0], (1, 2, 3, 4, 0)),
    )
    feats, edge = edges(sources, target, w1)
    halo = lax.ppermute(
        edge,
        ("aa", "ba"),
        [
            (a * blocks + i, (a ^ 1) * blocks + (i + 2 * (a % 2) - 1) % blocks)
            for a in range(size)
            for i in range(blocks)
        ],
    )
    ready, best, sums, near = inner(feats, target, edge, w1, w2, second_bias)
    own, mx = outer(blocks, near, halo, w1, w2, second_bias, sums, best, ready)
    other = lax.ppermute(own, "aa", [(i, i ^ 1) for i in range(size)])
    mx = lax.all_to_all(
        mx,
        ("aa", "ba"),
        0,
        0,
        tiled=True,
        axis_index_groups=[
            [(a + c) * blocks + i for c in range(2) for i in range(blocks)]
            for a in range(0, size, 2)
        ],
    )
    return finish(own, other, mx)


def solution(mesh):
    return jax.shard_map(
        per_device,
        mesh=mesh,
        in_specs=(P("aa", None, None), P("ba", None, None), P(), P(), P(), P()),
        out_specs=P("aa", None, "ba", None),
        check_vma=False,
    )
```

```python
import functools

import jax
import jax.numpy as jnp
from jax import lax
from jax.experimental import pallas as pl
from jax.experimental.pallas import tpu as pltpu
from jax.sharding import PartitionSpec as P

C = 1024
HID = 16
AW = 10
AR = 4
CELLS = AR * AW
PAIR = 24
PAD = 2 * PAIR
BW = 512
BR = 8
LINE = 80
HALF = 3 * LINE
GAP = 16
K1 = 2 * (HALF + GAP)
ROW = AW * HID
OWN = BR // 2
M1 = AR * ROW
M2 = 3 * CELLS
EPS = 1e-5
BF = jnp.bfloat16
F32 = jnp.float32
VMEM_LIMIT = 20 * 1024 * 1024


def cost(us):
    return pl.CostEstimate(flops=int(us * 1e9), bytes_accessed=int(us * 3e6), transcendentals=0)


def softplus(v):
    return jnp.maximum(v, 0.0) + jnp.log1p(jnp.exp(-jnp.abs(v)))


def shifted(x, t):
    if t == 1:
        return x
    lane = lax.broadcasted_iota(jnp.int32, x.shape, 1)
    if t == 0:
        return jnp.where(lane == 0, 0.0, pltpu.roll(x, 1, 1))
    return jnp.where(lane == BW - 1, 0.0, pltpu.roll(x, BW - 1, 1))


def table_kernel(out_ref):
    col = lax.broadcasted_iota(jnp.int32, (8, K1 // 2), 1)
    s = lax.shift_right_logical(col * 820, 16)
    rest = col - s * LINE
    t = lax.shift_right_logical(rest * 2731, 16)
    place = rest - t * PAIR
    real = (s < 3) & (t < 3)
    tap = s * 3 + t
    cell = jnp.where(real & (place < 2 * AW), place, -1000)
    one = jnp.where(real & (tap == 4) & (place >= 2 * AW), place - 2 * AW, -1000)
    row = lax.broadcasted_iota(jnp.int32, (8, K1 // 2), 0)
    out_ref[...] = jnp.where(row == 0, tap, jnp.where(row == 1, cell, one))


def tables():
    return pl.pallas_call(
        table_kernel,
        out_shape=jax.ShapeDtypeStruct((8, K1 // 2), jnp.int32),
        out_specs=pl.BlockSpec(memory_space=pltpu.VMEM),
        compiler_params=pltpu.CompilerParams(vmem_limit_bytes=4 * 1024 * 1024),
        cost_estimate=cost(4.0),
        name="tables",
    )()


def prep_kernel(table_ref, k1_ref, b1_ref, k2_ref, w1_ref, w2_ref, w2f_ref, flat_ref):
    me = lax.axis_index("aa")

    def lines(ref):
        for n in range(27):
            u, v, w = n // 9, n // 3 % 3, n % 3
            w = w if w == 1 else jnp.where(lax.rem(me, 2) == 0, w, 2 - w)
            flat_ref[3 * n : 3 * n + 3, :] = ref[u, v, w].astype(F32)
        return flat_ref[...].astype(BF)

    tap = table_ref[0:1, :]
    weight = lines(k1_ref)
    row_id = lax.broadcasted_iota(jnp.int32, (81, K1 // 2), 0)
    spread = []
    for uv in range(9):
        pick = jnp.where(row_id == uv * 9 + tap, 1.0, 0.0).astype(BF)
        spread.append(
            lax.dot_general(weight, pick, (((0,), (0,)), ((), ())), preferred_element_type=F32)
        )
    square = (HID, HID)
    on = lax.broadcasted_iota(jnp.int32, square, 0) == lax.broadcasted_iota(jnp.int32, square, 1)
    bias = jnp.sum(jnp.where(on, b1_ref[...], 0.0), axis=1, keepdims=True)
    hi = bias.astype(BF).astype(F32)
    mid = (bias - hi).astype(BF).astype(F32)
    low = bias - hi - mid
    one = jnp.broadcast_to(table_ref[2:3, :], (HID, K1 // 2))
    base = jnp.where(one == 0, hi, jnp.where(one == 1, mid, jnp.where(one == 2, low, 0.0)))
    cell = jnp.broadcast_to(table_ref[1:2, :], (HID, K1 // 2))
    for r in range(AR):
        for j in range(AW):
            for half in range(2):
                block = base if half == r // 3 else jnp.zeros_like(base)
                for u in range(3):
                    for v in range(3):
                        i = r + u - 1
                        if i // 2 == half and 0 <= j + v - 1 < AW:
                            where = i % 2 * AW + j + v - 1
                            block = jnp.where(cell == where, spread[u * 3 + v], block)
                start = (r * AW + j) * HID
                cut = slice(half * (K1 // 2), (half + 1) * (K1 // 2))
                w1_ref[start : start + HID, cut] = block.astype(BF)
    col = lax.broadcasted_iota(jnp.int32, (1, M1), 1)
    chan = lax.bitwise_and(col, HID - 1)
    pick = jnp.where(lax.broadcasted_iota(jnp.int32, (HID, M1), 0) == chan, 1.0, 0.0).astype(BF)
    rows = jnp.dot(lines(k2_ref), pick, preferred_element_type=F32)
    own = lax.broadcasted_iota(jnp.int32, (CELLS, M1), 0)
    own_row = jnp.where(own >= 10, 1, 0) + jnp.where(own >= 20, 1, 0) + jnp.where(own >= 30, 1, 0)
    own_col = own - own_row * AW
    own_cell = lax.bitwise_xor(own_row, me) * AW + own_col
    gap = lax.shift_right_logical(col, 4) - own_cell
    gaps = [
        jnp.where(own_col >= 1, gap, 1000),
        gap,
        jnp.where(own_col <= AW - 2, gap, 1000),
    ]
    for st in range(9):
        block = jnp.zeros((CELLS, M1), F32)
        for u in range(3):
            for v in range(3):
                n = (u * 3 + v) * 9 + st
                block = jnp.where(gaps[v] == (u - 1) * AW + v - 1, rows[n : n + 1, :], block)
        s, t = st // 3, st % 3
        w2f_ref[t * CELLS : (t + 1) * CELLS, s * M1 : (s + 1) * M1] = block
    w2_ref[...] = w2f_ref[...].astype(BF)


def prep(k1, b1, k2):
    vm = pl.BlockSpec(memory_space=pltpu.VMEM)
    return pl.pallas_call(
        prep_kernel,
        out_shape=(
            jax.ShapeDtypeStruct((M1, K1), BF),
            jax.ShapeDtypeStruct((M2, 3 * M1), BF),
        ),
        in_specs=[vm] * 4,
        out_specs=(vm, vm),
        scratch_shapes=[pltpu.VMEM((M2, 3 * M1), F32), pltpu.VMEM((81, HID), F32)],
        compiler_params=pltpu.CompilerParams(vmem_limit_bytes=VMEM_LIMIT),
        cost_estimate=cost(2.0),
        name="prep",
    )(tables(), k1, b1, k2)


def correlation(feats, block):
    product = lax.dot_general(
        feats, block, (((1,), (1,)), ((), ())), preferred_element_type=F32
    )
    value = (product * C ** (-0.5)).astype(BF).astype(F32)
    row = lax.broadcasted_iota(jnp.int32, value.shape, 0)
    filler = (row >= PAD - 4) | ((row >= PAIR - 4) & (row < PAIR))
    return jnp.where(filler, 1.0, value)


def target_row(target_ref, n):
    return target_ref[jnp.where(lax.rem(lax.axis_index("aa"), 2) == 0, n, BR - 1 - n)]


def edge_kernel(s0, s1, s2, s3, target_ref, w1_ref, feats_ref, edge_ref, stage):
    me = lax.axis_index("aa")
    given = [ref[0].astype(F32) for ref in (s0, s1, s2, s3)]
    stage[...] = jnp.zeros_like(stage)
    for n in range(AR):
        pick = given[n ^ 3]
        for k in range(3):
            pick = jnp.where(me == k, given[n ^ k], pick)
        start = n // 2 * PAIR + n % 2 * AW
        stage[start : start + AW, :] = pick
    feats = stage[...].astype(BF)
    feats_ref[...] = feats
    for n in range(2):
        value = correlation(feats, target_row(target_ref, n))
        edge_ref[:, n * BW : (n + 1) * BW] = value.astype(BF)


def edges(sources, target, w1):
    vm = pl.BlockSpec(memory_space=pltpu.VMEM)
    return pl.pallas_call(
        edge_kernel,
        out_shape=(
            jax.ShapeDtypeStruct((PAD, C), BF),
            jax.ShapeDtypeStruct((PAD, 2 * BW), BF),
        ),
        in_specs=[vm] * 5 + [pl.BlockSpec(memory_space=pl.ANY)],
        out_specs=(vm, vm),
        scratch_shapes=[pltpu.VMEM((PAD, C), F32)],
        compiler_params=pltpu.CompilerParams(vmem_limit_bytes=VMEM_LIMIT),
        cost_estimate=cost(2.0),
        name="edges",
    )(*sources, target, w1)


def three_shifts(value):
    moved = [shifted(value, t) for t in range(3)]
    fill = jnp.zeros((LINE - 3 * PAIR, BW), F32)
    return jnp.concatenate(
        [
            piece
            for n in range(2)
            for piece in (*(m[n * PAIR : (n + 1) * PAIR] for m in moved), fill)
        ],
        axis=0,
    ).astype(BF)


def hidden_row(w1_ref, parts, out_ref, start, drop=None):
    low = jnp.concatenate([part[0:LINE] for part in parts], axis=0)
    high = jnp.concatenate([part[LINE : 2 * LINE] for part in parts], axis=0)
    both = jnp.concatenate([low, jnp.zeros((GAP, BW), BF), high], axis=0)
    for first, rows, begin, x in (
        (0, ROW, 0, low),
        (ROW, 2 * ROW, 0, both),
        (3 * ROW, ROW, HALF + GAP, high),
    ):
        w1 = w1_ref[first : first + rows, begin : begin + x.shape[0]]
        value = jnp.maximum(jnp.dot(w1, x, preferred_element_type=F32), 0.0)
        if drop is not None:
            value = jnp.where(drop, 0.0, value)
        out_ref[start + first : start + first + rows, :] = value.astype(BF)


def sums_of(w2_ref, hidden_ref, s, first, count):
    return jnp.dot(
        w2_ref[:, s * M1 : (s + count) * M1],
        hidden_ref[first * M1 : (first + count) * M1, :],
        preferred_element_type=F32,
    )


def logit_row(sums, b2):
    return (
        sums[CELLS : 2 * CELLS, :]
        + shifted(sums[0:CELLS, :], 0)
        + shifted(sums[2 * CELLS : 3 * CELLS, :], 2)
        + b2
    )


def emit_row(logits, out_ref, n, best):
    mine = logits[0 : 2 * AW, :]
    out_ref[n, 0 : 2 * AW, :] = softplus(mine)
    top = jnp.max(logits, axis=0, keepdims=True)
    out_ref[n, 2 * AW : 2 * AW + 1, :] = softplus(top)
    return mine if best is None else jnp.maximum(best, mine)


def inner_kernel(
    feats_ref, target_ref, edge_ref, w1_ref, w2_ref, b2_ref,
    ready_ref, best_ref, sums_ref, near_ref, x, hidden,
):
    feats = feats_ref[...]
    for n in range(2):
        near_ref[n] = three_shifts(edge_ref[:, n * BW : (n + 1) * BW].astype(F32))
    for n in range(2, OWN + 2):
        x[n - 2] = three_shifts(correlation(feats, target_row(target_ref, n)))
    rows = [near_ref[0], near_ref[1], *(x[n] for n in range(OWN))]
    best = None
    for h in range(OWN):
        hidden_row(w1_ref, rows[h : h + 3], hidden, h * M1)
        if h >= 2:
            logits = logit_row(sums_of(w2_ref, hidden, 0, h - 2, 3), b2_ref[0])
            best = emit_row(logits, ready_ref, h - 2, best)
    best_ref[...] = best
    sums_ref[0] = sums_of(w2_ref, hidden, 2, 0, 1)
    sums_ref[1] = sums_of(w2_ref, hidden, 1, 0, 2)


def inner(feats, target, edge, w1, w2, b2):
    vm = pl.BlockSpec(memory_space=pltpu.VMEM)
    return pl.pallas_call(
        inner_kernel,
        out_shape=(
            jax.ShapeDtypeStruct((2, PAIR, BW), F32),
            jax.ShapeDtypeStruct((2 * AW, BW), F32),
            jax.ShapeDtypeStruct((2, M2, BW), F32),
            jax.ShapeDtypeStruct((2, 2 * LINE, BW), BF),
        ),
        in_specs=[vm] * 5 + [pl.BlockSpec(memory_space=pltpu.SMEM)],
        out_specs=(vm,) * 4,
        scratch_shapes=[
            pltpu.VMEM((OWN, 2 * LINE, BW), BF),
            pltpu.VMEM((OWN * M1, BW), BF),
        ],
        compiler_params=pltpu.CompilerParams(vmem_limit_bytes=VMEM_LIMIT),
        cost_estimate=cost(8.0),
        name="inner",
    )(feats, target, edge, w1, w2, b2)


def outer_kernel(
    blocks, near_ref, halo_ref, w1_ref, w2_ref, b2_ref, sums_ref, best_ref, inner_ref,
    out_ref, mx_ref, hidden,
):
    core = lax.rem(lax.axis_index("aa"), 2)
    outside = lax.axis_index("ba") == jnp.where(core == 0, 0, blocks - 1)
    rows = [
        three_shifts(jnp.where(outside, 0.0, halo_ref[:, n * BW : (n + 1) * BW].astype(F32)))
        for n in (1, 0)
    ] + [near_ref[0], near_ref[1]]
    hidden_row(w1_ref, rows[0:3], hidden, 0, outside)
    hidden_row(w1_ref, rows[1:4], hidden, M1)
    best = best_ref[...]
    for n in range(2):
        sums = sums_ref[n] + sums_of(w2_ref, hidden, 0, n, 2 - n)
        best = emit_row(logit_row(sums, b2_ref[0]), out_ref, n, best)
    out_ref[2:OWN] = inner_ref[...]
    top = jnp.max(best, axis=1, keepdims=True)
    row_id = lax.broadcasted_iota(jnp.int32, (2 * AW, 128), 0)
    lane = lax.broadcasted_iota(jnp.int32, (2 * AW, 128), 1)
    lines = [
        jnp.sum(jnp.where(row_id - n * AW == lane, top, 0.0), axis=0, keepdims=True)
        for n in range(2)
    ]
    lane = lane[0:1]
    lines = [jnp.where(lane < AW, line, 0.0) for line in lines]
    for n in range(2):
        line = jnp.where(core == n, lines[0], lines[1])
        mx_ref[n * blocks : (n + 1) * blocks, :] = jnp.broadcast_to(line, (blocks, 128))


def outer(blocks, near, halo, w1, w2, b2, sums, best, ready):
    vm = pl.BlockSpec(memory_space=pltpu.VMEM)
    return pl.pallas_call(
        functools.partial(outer_kernel, blocks),
        out_shape=(
            jax.ShapeDtypeStruct((OWN, PAIR, BW), F32),
            jax.ShapeDtypeStruct((2 * blocks, 128), F32),
        ),
        in_specs=[vm] * 4 + [pl.BlockSpec(memory_space=pltpu.SMEM)] + [vm] * 3,
        out_specs=(vm, vm),
        scratch_shapes=[pltpu.VMEM((2 * M1, BW), BF)],
        compiler_params=pltpu.CompilerParams(vmem_limit_bytes=VMEM_LIMIT),
        cost_estimate=cost(4.0),
        name="outer",
    )(near, halo, w1, w2, b2, sums, best, ready)


def final_kernel(own_ref, other_ref, mx_ref, out_ref):
    upper = lax.rem(lax.axis_index("aa"), 2) == 0
    top = softplus(jnp.max(mx_ref[...], axis=0, keepdims=True))
    row_id = lax.broadcasted_iota(jnp.int32, (AW, 128), 0)
    lane = lax.broadcasted_iota(jnp.int32, (AW, 128), 1)
    cell = jnp.sum(jnp.where(row_id == lane, top, 0.0), axis=1, keepdims=True) + EPS
    for p in range(BR):
        n = min(p, BR - 1 - p)
        here = upper if p < OWN else jnp.logical_not(upper)
        s = jnp.where(here, own_ref[n, 0:AW, :], other_ref[n, AW : 2 * AW, :])
        best = 2 * AW, 2 * AW + 1
        best = jnp.where(
            here, own_ref[n, best[0] : best[1], :], other_ref[n, best[0] : best[1], :]
        )
        value = s * (s / (best + EPS)) * (s / cell)
        for j in range(AW):
            out_ref[0, j, p : p + 1, :] = value[j : j + 1, :]


def finish(own, other, mx):
    vm = pl.BlockSpec(memory_space=pltpu.VMEM)
    return pl.pallas_call(
        final_kernel,
        out_shape=jax.ShapeDtypeStruct((1, AW, BR, BW), F32),
        in_specs=[vm] * 3,
        out_specs=vm,
        compiler_params=pltpu.CompilerParams(vmem_limit_bytes=4 * 1024 * 1024),
        name="finish",
    )(own, other, mx)


def neighbour(a, i, blocks):
    j = i + 2 * (a % 2) - 1
    return (a ^ 1) * blocks + j if 0 <= j < blocks else a * blocks + i


def per_device(source, target, first_kernel, first_bias, second_kernel, second_bias):
    blocks = lax.axis_size("ba")
    size = lax.axis_size("aa")
    sources = [source] + [
        lax.ppermute(source, "aa", [(i, i ^ k) for i in range(size)]) for k in range(1, size)
    ]
    w1, w2 = prep(
        jnp.transpose(first_kernel[:, 0], (1, 2, 3, 4, 0)),
        first_bias[None, :],
        jnp.transpose(second_kernel[0], (1, 2, 3, 4, 0)),
    )
    feats, edge = edges(sources, target, w1)
    halo = lax.ppermute(
        edge,
        ("aa", "ba"),
        [
            (a * blocks + i, neighbour(a, i, blocks))
            for a in range(size)
            for i in range(blocks)
        ],
    )
    ready, best, sums, near = inner(feats, target, edge, w1, w2, second_bias)
    own, mx = outer(blocks, near, halo, w1, w2, second_bias, sums, best, ready)
    other = lax.ppermute(own, "aa", [(i, i ^ 1) for i in range(size)])
    mx = lax.all_to_all(
        mx,
        ("aa", "ba"),
        0,
        0,
        tiled=True,
        axis_index_groups=[
            [(a + c) * blocks + i for c in range(2) for i in range(blocks)]
            for a in range(0, size, 2)
        ],
    )
    return finish(own, other, mx)


def solution(mesh):
    return jax.shard_map(
        per_device,
        mesh=mesh,
        in_specs=(P("aa", None, None), P("ba", None, None), P(), P(), P(), P()),
        out_specs=P("aa", None, "ba", None),
        check_vma=False,
    )
```

```python
import functools

import jax
import jax.numpy as jnp
from jax import lax
from jax.experimental import pallas as pl
from jax.experimental.pallas import tpu as pltpu
from jax.sharding import PartitionSpec as P

C = 1024
HID = 16
AW = 10
AR = 4
CELLS = AR * AW
PAIR = 24
PAD = 2 * PAIR
BW = 512
BR = 8
LINE = 80
HALF = 3 * LINE
GAP = 16
K1 = 2 * (HALF + GAP)
ROW = AW * HID
OWN = BR // 2
M1 = AR * ROW
M2 = 3 * CELLS
EPS = 1e-5
BF = jnp.bfloat16
F32 = jnp.float32
VMEM_LIMIT = 20 * 1024 * 1024


def cost(us):
    return pl.CostEstimate(flops=int(us * 1e9), bytes_accessed=int(us * 3e6), transcendentals=0)


def softplus(v):
    return jnp.maximum(v, 0.0) + jnp.log1p(jnp.exp(-jnp.abs(v)))


def shifted(x, t):
    if t == 1:
        return x
    lane = lax.broadcasted_iota(jnp.int32, x.shape, 1)
    if t == 0:
        return jnp.where(lane == 0, 0.0, pltpu.roll(x, 1, 1))
    return jnp.where(lane == BW - 1, 0.0, pltpu.roll(x, BW - 1, 1))


def table_kernel(out_ref):
    col = lax.broadcasted_iota(jnp.int32, (8, K1 // 2), 1)
    s = lax.shift_right_logical(col * 820, 16)
    rest = col - s * LINE
    t = lax.shift_right_logical(rest * 2731, 16)
    place = rest - t * PAIR
    real = (s < 3) & (t < 3)
    tap = s * 3 + t
    cell = jnp.where(real & (place < 2 * AW), place, -1000)
    one = jnp.where(real & (tap == 4) & (place >= 2 * AW), place - 2 * AW, -1000)
    row = lax.broadcasted_iota(jnp.int32, (8, K1 // 2), 0)
    out_ref[...] = jnp.where(row == 0, tap, jnp.where(row == 1, cell, one))


def tables():
    return pl.pallas_call(
        table_kernel,
        out_shape=jax.ShapeDtypeStruct((8, K1 // 2), jnp.int32),
        out_specs=pl.BlockSpec(memory_space=pltpu.VMEM),
        compiler_params=pltpu.CompilerParams(vmem_limit_bytes=4 * 1024 * 1024),
        cost_estimate=cost(4.0),
        name="tables",
    )()


def prep_kernel(table_ref, k1_ref, b1_ref, k2_ref, w1_ref, w2_ref, w2f_ref, flat_ref):
    me = lax.axis_index("aa")

    def lines(ref):
        for n in range(27):
            u, v, w = n // 9, n // 3 % 3, n % 3
            w = w if w == 1 else jnp.where(lax.rem(me, 2) == 0, w, 2 - w)
            flat_ref[3 * n : 3 * n + 3, :] = ref[u, v, w].astype(F32)
        return flat_ref[...].astype(BF)

    tap = table_ref[0:1, :]
    weight = lines(k1_ref)
    row_id = lax.broadcasted_iota(jnp.int32, (81, K1 // 2), 0)
    spread = []
    for uv in range(9):
        pick = jnp.where(row_id == uv * 9 + tap, 1.0, 0.0).astype(BF)
        spread.append(
            lax.dot_general(weight, pick, (((0,), (0,)), ((), ())), preferred_element_type=F32)
        )
    square = (HID, HID)
    on = lax.broadcasted_iota(jnp.int32, square, 0) == lax.broadcasted_iota(jnp.int32, square, 1)
    bias = jnp.sum(jnp.where(on, b1_ref[...], 0.0), axis=1, keepdims=True)
    hi = bias.astype(BF).astype(F32)
    mid = (bias - hi).astype(BF).astype(F32)
    low = bias - hi - mid
    one = jnp.broadcast_to(table_ref[2:3, :], (HID, K1 // 2))
    base = jnp.where(one == 0, hi, jnp.where(one == 1, mid, jnp.where(one == 2, low, 0.0)))
    cell = jnp.broadcast_to(table_ref[1:2, :], (HID, K1 // 2))
    for r in range(AR):
        for j in range(AW):
            for half in range(2):
                block = base if half == r // 3 else jnp.zeros_like(base)
                for u in range(3):
                    for v in range(3):
                        i = r + u - 1
                        if i // 2 == half and 0 <= j + v - 1 < AW:
                            where = i % 2 * AW + j + v - 1
                            block = jnp.where(cell == where, spread[u * 3 + v], block)
                start = (r * AW + j) * HID
                cut = slice(half * (K1 // 2), (half + 1) * (K1 // 2))
                w1_ref[start : start + HID, cut] = block.astype(BF)
    col = lax.broadcasted_iota(jnp.int32, (1, M1), 1)
    chan = lax.bitwise_and(col, HID - 1)
    pick = jnp.where(lax.broadcasted_iota(jnp.int32, (HID, M1), 0) == chan, 1.0, 0.0).astype(BF)
    rows = jnp.dot(lines(k2_ref), pick, preferred_element_type=F32)
    own = lax.broadcasted_iota(jnp.int32, (CELLS, M1), 0)
    own_row = jnp.where(own >= 10, 1, 0) + jnp.where(own >= 20, 1, 0) + jnp.where(own >= 30, 1, 0)
    own_col = own - own_row * AW
    own_cell = lax.bitwise_xor(own_row, me) * AW + own_col
    gap = lax.shift_right_logical(col, 4) - own_cell
    gaps = [
        jnp.where(own_col >= 1, gap, 1000),
        gap,
        jnp.where(own_col <= AW - 2, gap, 1000),
    ]
    for st in range(9):
        block = jnp.zeros((CELLS, M1), F32)
        for u in range(3):
            for v in range(3):
                n = (u * 3 + v) * 9 + st
                block = jnp.where(gaps[v] == (u - 1) * AW + v - 1, rows[n : n + 1, :], block)
        s, t = st // 3, st % 3
        w2f_ref[t * CELLS : (t + 1) * CELLS, s * M1 : (s + 1) * M1] = block
    w2_ref[...] = w2f_ref[...].astype(BF)


def prep(k1, b1, k2):
    vm = pl.BlockSpec(memory_space=pltpu.VMEM)
    return pl.pallas_call(
        prep_kernel,
        out_shape=(
            jax.ShapeDtypeStruct((M1, K1), BF),
            jax.ShapeDtypeStruct((M2, 3 * M1), BF),
        ),
        in_specs=[vm] * 4,
        out_specs=(vm, vm),
        scratch_shapes=[pltpu.VMEM((M2, 3 * M1), F32), pltpu.VMEM((81, HID), F32)],
        compiler_params=pltpu.CompilerParams(vmem_limit_bytes=VMEM_LIMIT),
        cost_estimate=cost(2.0),
        name="prep",
    )(tables(), k1, b1, k2)


def correlation(feats, block):
    product = lax.dot_general(
        feats, block, (((1,), (1,)), ((), ())), preferred_element_type=F32
    )
    value = (product * C ** (-0.5)).astype(BF).astype(F32)
    row = lax.broadcasted_iota(jnp.int32, value.shape, 0)
    filler = (row >= PAD - 4) | ((row >= PAIR - 4) & (row < PAIR))
    return jnp.where(filler, 1.0, value)


def target_row(target_ref, n):
    return target_ref[jnp.where(lax.rem(lax.axis_index("aa"), 2) == 0, n, BR - 1 - n)]


def edge_kernel(s0, s1, s2, s3, target_ref, w1_ref, feats_ref, edge_ref, stage):
    me = lax.axis_index("aa")
    given = [ref[0].astype(F32) for ref in (s0, s1, s2, s3)]
    stage[...] = jnp.zeros_like(stage)
    for n in range(AR):
        pick = given[n ^ 3]
        for k in range(3):
            pick = jnp.where(me == k, given[n ^ k], pick)
        start = n // 2 * PAIR + n % 2 * AW
        stage[start : start + AW, :] = pick
    feats = stage[...].astype(BF)
    feats_ref[...] = feats
    for n in range(2):
        value = correlation(feats, target_row(target_ref, n))
        edge_ref[:, n * BW : (n + 1) * BW] = value.astype(BF)


def edges(sources, target, w1):
    vm = pl.BlockSpec(memory_space=pltpu.VMEM)
    return pl.pallas_call(
        edge_kernel,
        out_shape=(
            jax.ShapeDtypeStruct((PAD, C), BF),
            jax.ShapeDtypeStruct((PAD, 2 * BW), BF),
        ),
        in_specs=[vm] * 5 + [pl.BlockSpec(memory_space=pl.ANY)],
        out_specs=(vm, vm),
        scratch_shapes=[pltpu.VMEM((PAD, C), F32)],
        compiler_params=pltpu.CompilerParams(vmem_limit_bytes=VMEM_LIMIT),
        cost_estimate=cost(2.0),
        name="edges",
    )(*sources, target, w1)


def three_shifts(value):
    moved = [shifted(value, t) for t in range(3)]
    fill = jnp.zeros((LINE - 3 * PAIR, BW), F32)
    return jnp.concatenate(
        [
            piece
            for n in range(2)
            for piece in (*(m[n * PAIR : (n + 1) * PAIR] for m in moved), fill)
        ],
        axis=0,
    ).astype(BF)


def hidden_row(w1_ref, parts, out_ref, start, drop=None):
    low = jnp.concatenate([part[0:LINE] for part in parts], axis=0)
    high = jnp.concatenate([part[LINE : 2 * LINE] for part in parts], axis=0)
    both = jnp.concatenate([low, jnp.zeros((GAP, BW), BF), high], axis=0)
    for first, rows, begin, x in (
        (0, ROW, 0, low),
        (ROW, 2 * ROW, 0, both),
        (3 * ROW, ROW, HALF + GAP, high),
    ):
        w1 = w1_ref[first : first + rows, begin : begin + x.shape[0]]
        value = jnp.maximum(jnp.dot(w1, x, preferred_element_type=F32), 0.0)
        if drop is not None:
            value = jnp.where(drop, 0.0, value)
        out_ref[start + first : start + first + rows, :] = value.astype(BF)


def sums_of(w2_ref, hidden_ref, s, first, count):
    return jnp.dot(
        w2_ref[:, s * M1 : (s + count) * M1],
        hidden_ref[first * M1 : (first + count) * M1, :],
        preferred_element_type=F32,
    )


def logit_row(sums, b2):
    return (
        sums[CELLS : 2 * CELLS, :]
        + shifted(sums[0:CELLS, :], 0)
        + shifted(sums[2 * CELLS : 3 * CELLS, :], 2)
        + b2
    )


def emit_row(logits, out_ref, n, best):
    mine = logits[0 : 2 * AW, :]
    out_ref[n, 0 : 2 * AW, :] = softplus(mine)
    top = jnp.max(logits, axis=0, keepdims=True)
    out_ref[n, 2 * AW : 2 * AW + 1, :] = softplus(top)
    return mine if best is None else jnp.maximum(best, mine)


def inner_kernel(
    feats_ref, target_ref, edge_ref, w1_ref, w2_ref, b2_ref,
    ready_ref, best_ref, sums_ref, near_ref, x, hidden,
):
    feats = feats_ref[...]
    for n in range(2):
        near_ref[n] = three_shifts(edge_ref[:, n * BW : (n + 1) * BW].astype(F32))
    for n in range(2, OWN + 2):
        x[n - 2] = three_shifts(correlation(feats, target_row(target_ref, n)))
    rows = [near_ref[0], near_ref[1], *(x[n] for n in range(OWN))]
    best = None
    for h in range(OWN):
        hidden_row(w1_ref, rows[h : h + 3], hidden, h * M1)
        if h >= 2:
            logits = logit_row(sums_of(w2_ref, hidden, 0, h - 2, 3), b2_ref[0])
            best = emit_row(logits, ready_ref, h - 2, best)
    best_ref[...] = best
    sums_ref[0] = sums_of(w2_ref, hidden, 2, 0, 1)
    sums_ref[1] = sums_of(w2_ref, hidden, 1, 0, 2)


def inner(feats, target, edge, w1, w2, b2):
    vm = pl.BlockSpec(memory_space=pltpu.VMEM)
    return pl.pallas_call(
        inner_kernel,
        out_shape=(
            jax.ShapeDtypeStruct((2, PAIR, BW), F32),
            jax.ShapeDtypeStruct((2 * AW, BW), F32),
            jax.ShapeDtypeStruct((2, M2, BW), F32),
            jax.ShapeDtypeStruct((2, 2 * LINE, BW), BF),
        ),
        in_specs=[vm] * 5 + [pl.BlockSpec(memory_space=pltpu.SMEM)],
        out_specs=(vm,) * 4,
        scratch_shapes=[
            pltpu.VMEM((OWN, 2 * LINE, BW), BF),
            pltpu.VMEM((OWN * M1, BW), BF),
        ],
        compiler_params=pltpu.CompilerParams(vmem_limit_bytes=VMEM_LIMIT),
        cost_estimate=cost(8.0),
        name="inner",
    )(feats, target, edge, w1, w2, b2)


def outer_kernel(
    blocks, near_ref, halo_ref, w1_ref, w2_ref, b2_ref, sums_ref, best_ref, inner_ref,
    out_ref, mx_ref, hidden,
):
    core = lax.rem(lax.axis_index("aa"), 2)
    outside = lax.axis_index("ba") == jnp.where(core == 0, 0, blocks - 1)
    rows = [
        three_shifts(jnp.where(outside, 0.0, halo_ref[:, n * BW : (n + 1) * BW].astype(F32)))
        for n in (1, 0)
    ] + [near_ref[0], near_ref[1]]
    hidden_row(w1_ref, rows[0:3], hidden, 0, outside)
    hidden_row(w1_ref, rows[1:4], hidden, M1)
    best = best_ref[...]
    for n in range(2):
        sums = sums_ref[n] + sums_of(w2_ref, hidden, 0, n, 2 - n)
        best = emit_row(logit_row(sums, b2_ref[0]), out_ref, n, best)
    out_ref[2:OWN] = inner_ref[...]
    top = jnp.max(best, axis=1, keepdims=True)
    row_id = lax.broadcasted_iota(jnp.int32, (2 * AW, 128), 0)
    lane = lax.broadcasted_iota(jnp.int32, (2 * AW, 128), 1)
    lines = [
        jnp.sum(jnp.where(row_id - n * AW == lane, top, 0.0), axis=0, keepdims=True)
        for n in range(2)
    ]
    lane = lane[0:1]
    lines = [jnp.where(lane < AW, line, 0.0) for line in lines]
    for n in range(2):
        line = jnp.where(core == n, lines[0], lines[1])
        mx_ref[n * blocks : (n + 1) * blocks, :] = jnp.broadcast_to(line, (blocks, 128))


def outer(blocks, near, halo, w1, w2, b2, sums, best, ready):
    vm = pl.BlockSpec(memory_space=pltpu.VMEM)
    return pl.pallas_call(
        functools.partial(outer_kernel, blocks),
        out_shape=(
            jax.ShapeDtypeStruct((OWN, PAIR, BW), F32),
            jax.ShapeDtypeStruct((2 * blocks, 128), F32),
        ),
        in_specs=[vm] * 4 + [pl.BlockSpec(memory_space=pltpu.SMEM)] + [vm] * 3,
        out_specs=(vm, vm),
        scratch_shapes=[pltpu.VMEM((2 * M1, BW), BF)],
        compiler_params=pltpu.CompilerParams(vmem_limit_bytes=VMEM_LIMIT),
        cost_estimate=cost(4.0),
        name="outer",
    )(near, halo, w1, w2, b2, sums, best, ready)


def final_kernel(own_ref, other_ref, mx_ref, out_ref):
    upper = lax.rem(lax.axis_index("aa"), 2) == 0
    top = softplus(jnp.max(mx_ref[...], axis=0, keepdims=True))
    row_id = lax.broadcasted_iota(jnp.int32, (AW, 128), 0)
    lane = lax.broadcasted_iota(jnp.int32, (AW, 128), 1)
    cell = jnp.sum(jnp.where(row_id == lane, top, 0.0), axis=1, keepdims=True) + EPS
    for p in range(BR):
        n = min(p, BR - 1 - p)
        here = upper if p < OWN else jnp.logical_not(upper)
        s = jnp.where(here, own_ref[n, 0:AW, :], other_ref[n, AW : 2 * AW, :])
        best = 2 * AW, 2 * AW + 1
        best = jnp.where(
            here, own_ref[n, best[0] : best[1], :], other_ref[n, best[0] : best[1], :]
        )
        value = s * (s / (best + EPS)) * (s / cell)
        for j in range(AW):
            out_ref[0, j, p : p + 1, :] = value[j : j + 1, :]


def finish(own, other, mx):
    vm = pl.BlockSpec(memory_space=pltpu.VMEM)
    return pl.pallas_call(
        final_kernel,
        out_shape=jax.ShapeDtypeStruct((1, AW, BR, BW), F32),
        in_specs=[vm] * 3,
        out_specs=vm,
        compiler_params=pltpu.CompilerParams(vmem_limit_bytes=4 * 1024 * 1024),
        name="finish",
    )(own, other, mx)


def neighbour(a, i, blocks):
    j = i + 2 * (a % 2) - 1
    return (a ^ 1) * blocks + j if 0 <= j < blocks else (a ^ 2) * blocks + i


def per_device(source, target, first_kernel, first_bias, second_kernel, second_bias):
    blocks = lax.axis_size("ba")
    size = lax.axis_size("aa")
    sources = [source] + [
        lax.ppermute(source, "aa", [(i, i ^ k) for i in range(size)]) for k in range(1, size)
    ]
    w1, w2 = prep(
        jnp.transpose(first_kernel[:, 0], (1, 2, 3, 4, 0)),
        first_bias[None, :],
        jnp.transpose(second_kernel[0], (1, 2, 3, 4, 0)),
    )
    feats, edge = edges(sources, target, w1)
    halo = lax.ppermute(
        edge,
        ("aa", "ba"),
        [
            (a * blocks + i, neighbour(a, i, blocks))
            for a in range(size)
            for i in range(blocks)
        ],
    )
    ready, best, sums, near = inner(feats, target, edge, w1, w2, second_bias)
    own, mx = outer(blocks, near, halo, w1, w2, second_bias, sums, best, ready)
    other = lax.ppermute(own, "aa", [(i, i ^ 1) for i in range(size)])
    mx = lax.all_to_all(
        mx,
        ("aa", "ba"),
        0,
        0,
        tiled=True,
        axis_index_groups=[
            [(a + c) * blocks + i for c in range(2) for i in range(blocks)]
            for a in range(0, size, 2)
        ],
    )
    return finish(own, other, mx)


def solution(mesh):
    return jax.shard_map(
        per_device,
        mesh=mesh,
        in_specs=(P("aa", None, None), P("ba", None, None), P(), P(), P(), P()),
        out_specs=P("aa", None, "ba", None),
        check_vma=False,
    )
```

```python
import functools

import jax
import jax.numpy as jnp
from jax import lax
from jax.experimental import pallas as pl
from jax.experimental.pallas import tpu as pltpu
from jax.sharding import PartitionSpec as P

C = 1024
HID = 16
AW = 10
AR = 4
CELLS = AR * AW
PAIR = 24
PAD = 2 * PAIR
BW = 512
BR = 8
LINE = 80
HALF = 3 * LINE
GAP = 16
K1 = 2 * (HALF + GAP)
ROW = AW * HID
OWN = BR // 2
M1 = AR * ROW
M2 = 3 * CELLS
EPS = 1e-5
BF = jnp.bfloat16
F32 = jnp.float32
VMEM_LIMIT = 20 * 1024 * 1024


def cost(us):
    return pl.CostEstimate(flops=int(us * 1e9), bytes_accessed=int(us * 3e6), transcendentals=0)


def softplus(v):
    return jnp.maximum(v, 0.0) + jnp.log1p(jnp.exp(-jnp.abs(v)))


def shifted(x, t):
    if t == 1:
        return x
    lane = lax.broadcasted_iota(jnp.int32, x.shape, 1)
    if t == 0:
        return jnp.where(lane == 0, 0.0, pltpu.roll(x, 1, 1))
    return jnp.where(lane == BW - 1, 0.0, pltpu.roll(x, BW - 1, 1))


def table_kernel(out_ref):
    col = lax.broadcasted_iota(jnp.int32, (8, K1 // 2), 1)
    s = lax.shift_right_logical(col * 820, 16)
    rest = col - s * LINE
    t = lax.shift_right_logical(rest * 2731, 16)
    place = rest - t * PAIR
    real = (s < 3) & (t < 3)
    tap = s * 3 + t
    cell = jnp.where(real & (place < 2 * AW), place, -1000)
    one = jnp.where(real & (tap == 4) & (place >= 2 * AW), place - 2 * AW, -1000)
    row = lax.broadcasted_iota(jnp.int32, (8, K1 // 2), 0)
    out_ref[...] = jnp.where(row == 0, tap, jnp.where(row == 1, cell, one))


def tables():
    return pl.pallas_call(
        table_kernel,
        out_shape=jax.ShapeDtypeStruct((8, K1 // 2), jnp.int32),
        out_specs=pl.BlockSpec(memory_space=pltpu.VMEM),
        compiler_params=pltpu.CompilerParams(vmem_limit_bytes=4 * 1024 * 1024),
        cost_estimate=cost(4.0),
        name="tables",
    )()


def prep_kernel(table_ref, k1_ref, b1_ref, k2_ref, w1_ref, w2_ref, w2f_ref, flat_ref):
    me = lax.axis_index("aa")

    def lines(ref):
        for n in range(27):
            u, v, w = n // 9, n // 3 % 3, n % 3
            w = w if w == 1 else jnp.where(lax.rem(me, 2) == 0, w, 2 - w)
            flat_ref[3 * n : 3 * n + 3, :] = ref[u, v, w].astype(F32)
        return flat_ref[...].astype(BF)

    tap = table_ref[0:1, :]
    weight = lines(k1_ref)
    row_id = lax.broadcasted_iota(jnp.int32, (81, K1 // 2), 0)
    spread = []
    for uv in range(9):
        pick = jnp.where(row_id == uv * 9 + tap, 1.0, 0.0).astype(BF)
        spread.append(
            lax.dot_general(weight, pick, (((0,), (0,)), ((), ())), preferred_element_type=F32)
        )
    square = (HID, HID)
    on = lax.broadcasted_iota(jnp.int32, square, 0) == lax.broadcasted_iota(jnp.int32, square, 1)
    bias = jnp.sum(jnp.where(on, b1_ref[...], 0.0), axis=1, keepdims=True)
    hi = bias.astype(BF).astype(F32)
    mid = (bias - hi).astype(BF).astype(F32)
    low = bias - hi - mid
    one = jnp.broadcast_to(table_ref[2:3, :], (HID, K1 // 2))
    base = jnp.where(one == 0, hi, jnp.where(one == 1, mid, jnp.where(one == 2, low, 0.0)))
    cell = jnp.broadcast_to(table_ref[1:2, :], (HID, K1 // 2))
    for r in range(AR):
        for j in range(AW):
            for half in range(2):
                block = base if half == r // 3 else jnp.zeros_like(base)
                for u in range(3):
                    for v in range(3):
                        i = r + u - 1
                        if i // 2 == half and 0 <= j + v - 1 < AW:
                            where = i % 2 * AW + j + v - 1
                            block = jnp.where(cell == where, spread[u * 3 + v], block)
                start = (r * AW + j) * HID
                cut = slice(half * (K1 // 2), (half + 1) * (K1 // 2))
                w1_ref[start : start + HID, cut] = block.astype(BF)
    col = lax.broadcasted_iota(jnp.int32, (1, M1), 1)
    chan = lax.bitwise_and(col, HID - 1)
    pick = jnp.where(lax.broadcasted_iota(jnp.int32, (HID, M1), 0) == chan, 1.0, 0.0).astype(BF)
    rows = jnp.dot(lines(k2_ref), pick, preferred_element_type=F32)
    own = lax.broadcasted_iota(jnp.int32, (CELLS, M1), 0)
    own_row = jnp.where(own >= 10, 1, 0) + jnp.where(own >= 20, 1, 0) + jnp.where(own >= 30, 1, 0)
    own_col = own - own_row * AW
    own_cell = lax.bitwise_xor(own_row, me) * AW + own_col
    gap = lax.shift_right_logical(col, 4) - own_cell
    gaps = [
        jnp.where(own_col >= 1, gap, 1000),
        gap,
        jnp.where(own_col <= AW - 2, gap, 1000),
    ]
    for st in range(9):
        block = jnp.zeros((CELLS, M1), F32)
        for u in range(3):
            for v in range(3):
                n = (u * 3 + v) * 9 + st
                block = jnp.where(gaps[v] == (u - 1) * AW + v - 1, rows[n : n + 1, :], block)
        s, t = st // 3, st % 3
        w2f_ref[t * CELLS : (t + 1) * CELLS, s * M1 : (s + 1) * M1] = block
    w2_ref[...] = w2f_ref[...].astype(BF)


def prep(k1, b1, k2):
    vm = pl.BlockSpec(memory_space=pltpu.VMEM)
    return pl.pallas_call(
        prep_kernel,
        out_shape=(
            jax.ShapeDtypeStruct((M1, K1), BF),
            jax.ShapeDtypeStruct((M2, 3 * M1), BF),
        ),
        in_specs=[vm] * 4,
        out_specs=(vm, vm),
        scratch_shapes=[pltpu.VMEM((M2, 3 * M1), F32), pltpu.VMEM((81, HID), F32)],
        compiler_params=pltpu.CompilerParams(vmem_limit_bytes=VMEM_LIMIT),
        cost_estimate=cost(2.0),
        name="prep",
    )(tables(), k1, b1, k2)


def correlation(feats, block):
    product = lax.dot_general(
        feats, block, (((1,), (1,)), ((), ())), preferred_element_type=F32
    )
    value = (product * C ** (-0.5)).astype(BF).astype(F32)
    row = lax.broadcasted_iota(jnp.int32, value.shape, 0)
    filler = (row >= PAD - 4) | ((row >= PAIR - 4) & (row < PAIR))
    return jnp.where(filler, 1.0, value)


def target_row(target_ref, n):
    return target_ref[jnp.where(lax.rem(lax.axis_index("aa"), 2) == 0, n, BR - 1 - n)]


def edge_kernel(s0, s1, s3, s2, target_ref, w1_ref, feats_ref, edge_ref, stage):
    me = lax.axis_index("aa")
    given = [ref[0].astype(F32) for ref in (s0, s1, s2, s3)]
    stage[...] = jnp.zeros_like(stage)
    for n in range(AR):
        pick = given[n ^ 3]
        for k in range(3):
            pick = jnp.where(me == k, given[n ^ k], pick)
        start = n // 2 * PAIR + n % 2 * AW
        stage[start : start + AW, :] = pick
    feats = stage[...].astype(BF)
    feats_ref[...] = feats
    for n in range(2):
        value = correlation(feats, target_row(target_ref, n))
        edge_ref[:, n * BW : (n + 1) * BW] = value.astype(BF)


def edges(sources, target, w1):
    vm = pl.BlockSpec(memory_space=pltpu.VMEM)
    return pl.pallas_call(
        edge_kernel,
        out_shape=(
            jax.ShapeDtypeStruct((PAD, C), BF),
            jax.ShapeDtypeStruct((PAD, 2 * BW), BF),
        ),
        in_specs=[vm] * 5 + [pl.BlockSpec(memory_space=pl.ANY)],
        out_specs=(vm, vm),
        scratch_shapes=[pltpu.VMEM((PAD, C), F32)],
        compiler_params=pltpu.CompilerParams(vmem_limit_bytes=VMEM_LIMIT),
        cost_estimate=cost(2.0),
        name="edges",
    )(sources[0], sources[1], sources[3], sources[2], target, w1)


def three_shifts(value):
    moved = [shifted(value, t) for t in range(3)]
    fill = jnp.zeros((LINE - 3 * PAIR, BW), F32)
    return jnp.concatenate(
        [
            piece
            for n in range(2)
            for piece in (*(m[n * PAIR : (n + 1) * PAIR] for m in moved), fill)
        ],
        axis=0,
    ).astype(BF)


def hidden_row(w1_ref, parts, out_ref, start, drop=None):
    low = jnp.concatenate([part[0:LINE] for part in parts], axis=0)
    high = jnp.concatenate([part[LINE : 2 * LINE] for part in parts], axis=0)
    both = jnp.concatenate([low, jnp.zeros((GAP, BW), BF), high], axis=0)
    for first, rows, begin, x in (
        (0, ROW, 0, low),
        (ROW, 2 * ROW, 0, both),
        (3 * ROW, ROW, HALF + GAP, high),
    ):
        w1 = w1_ref[first : first + rows, begin : begin + x.shape[0]]
        value = jnp.maximum(jnp.dot(w1, x, preferred_element_type=F32), 0.0)
        if drop is not None:
            value = jnp.where(drop, 0.0, value)
        out_ref[start + first : start + first + rows, :] = value.astype(BF)


def sums_of(w2_ref, hidden_ref, s, first, count):
    return jnp.dot(
        w2_ref[:, s * M1 : (s + count) * M1],
        hidden_ref[first * M1 : (first + count) * M1, :],
        preferred_element_type=F32,
    )


def logit_row(sums, b2):
    return (
        sums[CELLS : 2 * CELLS, :]
        + shifted(sums[0:CELLS, :], 0)
        + shifted(sums[2 * CELLS : 3 * CELLS, :], 2)
        + b2
    )


def emit_row(logits, out_ref, n, best):
    mine = logits[0 : 2 * AW, :]
    out_ref[n, 0 : 2 * AW, :] = softplus(mine)
    top = jnp.max(logits, axis=0, keepdims=True)
    out_ref[n, 2 * AW : 2 * AW + 1, :] = softplus(top)
    return mine if best is None else jnp.maximum(best, mine)


def inner_kernel(
    feats_ref, target_ref, edge_ref, w1_ref, w2_ref, b2_ref,
    ready_ref, best_ref, sums_ref, near_ref, x, hidden,
):
    feats = feats_ref[...]
    for n in range(2):
        near_ref[n] = three_shifts(edge_ref[:, n * BW : (n + 1) * BW].astype(F32))
    for n in range(2, OWN + 2):
        x[n - 2] = three_shifts(correlation(feats, target_row(target_ref, n)))
    rows = [near_ref[0], near_ref[1], *(x[n] for n in range(OWN))]
    best = None
    for h in range(OWN):
        hidden_row(w1_ref, rows[h : h + 3], hidden, h * M1)
        if h >= 2:
            logits = logit_row(sums_of(w2_ref, hidden, 0, h - 2, 3), b2_ref[0])
            best = emit_row(logits, ready_ref, h - 2, best)
    best_ref[...] = best
    sums_ref[0] = sums_of(w2_ref, hidden, 2, 0, 1)
    sums_ref[1] = sums_of(w2_ref, hidden, 1, 0, 2)


def inner(feats, target, edge, w1, w2, b2):
    vm = pl.BlockSpec(memory_space=pltpu.VMEM)
    return pl.pallas_call(
        inner_kernel,
        out_shape=(
            jax.ShapeDtypeStruct((2, PAIR, BW), F32),
            jax.ShapeDtypeStruct((2 * AW, BW), F32),
            jax.ShapeDtypeStruct((2, M2, BW), F32),
            jax.ShapeDtypeStruct((2, 2 * LINE, BW), BF),
        ),
        in_specs=[vm] * 5 + [pl.BlockSpec(memory_space=pltpu.SMEM)],
        out_specs=(vm,) * 4,
        scratch_shapes=[
            pltpu.VMEM((OWN, 2 * LINE, BW), BF),
            pltpu.VMEM((OWN * M1, BW), BF),
        ],
        compiler_params=pltpu.CompilerParams(vmem_limit_bytes=VMEM_LIMIT),
        cost_estimate=cost(8.0),
        name="inner",
    )(feats, target, edge, w1, w2, b2)


def outer_kernel(
    blocks, near_ref, halo_ref, w1_ref, w2_ref, b2_ref, sums_ref, best_ref, inner_ref,
    out_ref, mx_ref, hidden,
):
    core = lax.rem(lax.axis_index("aa"), 2)
    outside = lax.axis_index("ba") == jnp.where(core == 0, 0, blocks - 1)
    rows = [
        three_shifts(jnp.where(outside, 0.0, halo_ref[:, n * BW : (n + 1) * BW].astype(F32)))
        for n in (1, 0)
    ] + [near_ref[0], near_ref[1]]
    hidden_row(w1_ref, rows[0:3], hidden, 0, outside)
    hidden_row(w1_ref, rows[1:4], hidden, M1)
    best = best_ref[...]
    for n in range(2):
        sums = sums_ref[n] + sums_of(w2_ref, hidden, 0, n, 2 - n)
        best = emit_row(logit_row(sums, b2_ref[0]), out_ref, n, best)
    out_ref[2:OWN] = inner_ref[...]
    top = jnp.max(best, axis=1, keepdims=True)
    row_id = lax.broadcasted_iota(jnp.int32, (2 * AW, 128), 0)
    lane = lax.broadcasted_iota(jnp.int32, (2 * AW, 128), 1)
    lines = [
        jnp.sum(jnp.where(row_id - n * AW == lane, top, 0.0), axis=0, keepdims=True)
        for n in range(2)
    ]
    lane = lane[0:1]
    lines = [jnp.where(lane < AW, line, 0.0) for line in lines]
    for n in range(2):
        line = jnp.where(core == n, lines[0], lines[1])
        mx_ref[n * blocks : (n + 1) * blocks, :] = jnp.broadcast_to(line, (blocks, 128))


def outer(blocks, near, halo, w1, w2, b2, sums, best, ready):
    vm = pl.BlockSpec(memory_space=pltpu.VMEM)
    return pl.pallas_call(
        functools.partial(outer_kernel, blocks),
        out_shape=(
            jax.ShapeDtypeStruct((OWN, PAIR, BW), F32),
            jax.ShapeDtypeStruct((2 * blocks, 128), F32),
        ),
        in_specs=[vm] * 4 + [pl.BlockSpec(memory_space=pltpu.SMEM)] + [vm] * 3,
        out_specs=(vm, vm),
        scratch_shapes=[pltpu.VMEM((2 * M1, BW), BF)],
        compiler_params=pltpu.CompilerParams(vmem_limit_bytes=VMEM_LIMIT),
        cost_estimate=cost(4.0),
        name="outer",
    )(near, halo, w1, w2, b2, sums, best, ready)


def final_kernel(own_ref, other_ref, mx_ref, out_ref):
    upper = lax.rem(lax.axis_index("aa"), 2) == 0
    top = softplus(jnp.max(mx_ref[...], axis=0, keepdims=True))
    row_id = lax.broadcasted_iota(jnp.int32, (AW, 128), 0)
    lane = lax.broadcasted_iota(jnp.int32, (AW, 128), 1)
    cell = jnp.sum(jnp.where(row_id == lane, top, 0.0), axis=1, keepdims=True) + EPS
    for p in range(BR):
        n = min(p, BR - 1 - p)
        here = upper if p < OWN else jnp.logical_not(upper)
        s = jnp.where(here, own_ref[n, 0:AW, :], other_ref[n, AW : 2 * AW, :])
        best = 2 * AW, 2 * AW + 1
        best = jnp.where(
            here, own_ref[n, best[0] : best[1], :], other_ref[n, best[0] : best[1], :]
        )
        value = s * (s / (best + EPS)) * (s / cell)
        for j in range(AW):
            out_ref[0, j, p : p + 1, :] = value[j : j + 1, :]


def finish(own, other, mx):
    vm = pl.BlockSpec(memory_space=pltpu.VMEM)
    return pl.pallas_call(
        final_kernel,
        out_shape=jax.ShapeDtypeStruct((1, AW, BR, BW), F32),
        in_specs=[vm] * 3,
        out_specs=vm,
        compiler_params=pltpu.CompilerParams(vmem_limit_bytes=4 * 1024 * 1024),
        name="finish",
    )(own, other, mx)


def neighbour(a, i, blocks):
    j = i + 2 * (a % 2) - 1
    return (a ^ 1) * blocks + j if 0 <= j < blocks else (a ^ 2) * blocks + i


def per_device(source, target, first_kernel, first_bias, second_kernel, second_bias):
    blocks = lax.axis_size("ba")
    size = lax.axis_size("aa")
    sources = [source] + [
        lax.ppermute(source, "aa", [(i, i ^ k) for i in range(size)]) for k in range(1, size)
    ]
    w1, w2 = prep(
        jnp.transpose(first_kernel[:, 0], (1, 2, 3, 4, 0)),
        first_bias[None, :],
        jnp.transpose(second_kernel[0], (1, 2, 3, 4, 0)),
    )
    feats, edge = edges(sources, target, w1)
    halo = lax.ppermute(
        edge,
        ("aa", "ba"),
        [
            (a * blocks + i, neighbour(a, i, blocks))
            for a in range(size)
            for i in range(blocks)
        ],
    )
    ready, best, sums, near = inner(feats, target, edge, w1, w2, second_bias)
    own, mx = outer(blocks, near, halo, w1, w2, second_bias, sums, best, ready)
    other = lax.ppermute(own, "aa", [(i, i ^ 1) for i in range(size)])
    mx = lax.all_to_all(
        mx,
        ("aa", "ba"),
        0,
        0,
        tiled=True,
        axis_index_groups=[
            [(a + c) * blocks + i for c in range(2) for i in range(blocks)]
            for a in range(0, size, 2)
        ],
    )
    return finish(own, other, mx)


def solution(mesh):
    return jax.shard_map(
        per_device,
        mesh=mesh,
        in_specs=(P("aa", None, None), P("ba", None, None), P(), P(), P(), P()),
        out_specs=P("aa", None, "ba", None),
        check_vma=False,
    )
```

```python
import functools

import jax
import jax.numpy as jnp
from jax import lax
from jax.experimental import pallas as pl
from jax.experimental.pallas import tpu as pltpu
from jax.sharding import PartitionSpec as P

C = 1024
HID = 16
AW = 10
AR = 4
CELLS = AR * AW
PAIR = 24
PAD = 2 * PAIR
BW = 512
BR = 8
LINE = 80
HALF = 3 * LINE
GAP = 16
K1 = 2 * (HALF + GAP)
ROW = AW * HID
OWN = BR // 2
M1 = AR * ROW
M2 = 3 * CELLS
EPS = 1e-5
BF = jnp.bfloat16
F32 = jnp.float32
VMEM_LIMIT = 20 * 1024 * 1024


def cost(us):
    return pl.CostEstimate(flops=int(us * 1e9), bytes_accessed=int(us * 3e6), transcendentals=0)


def softplus(v):
    return jnp.maximum(v, 0.0) + jnp.log1p(jnp.exp(-jnp.abs(v)))


def shifted(x, t):
    if t == 1:
        return x
    lane = lax.broadcasted_iota(jnp.int32, x.shape, 1)
    if t == 0:
        return jnp.where(lane == 0, 0.0, pltpu.roll(x, 1, 1))
    return jnp.where(lane == BW - 1, 0.0, pltpu.roll(x, BW - 1, 1))


def table_kernel(out_ref):
    col = lax.broadcasted_iota(jnp.int32, (8, K1 // 2), 1)
    s = lax.shift_right_logical(col * 820, 16)
    rest = col - s * LINE
    t = lax.shift_right_logical(rest * 2731, 16)
    place = rest - t * PAIR
    real = (s < 3) & (t < 3)
    tap = s * 3 + t
    cell = jnp.where(real & (place < 2 * AW), place, -1000)
    one = jnp.where(real & (tap == 4) & (place >= 2 * AW), place - 2 * AW, -1000)
    row = lax.broadcasted_iota(jnp.int32, (8, K1 // 2), 0)
    out_ref[...] = jnp.where(row == 0, tap, jnp.where(row == 1, cell, one))


def tables():
    return pl.pallas_call(
        table_kernel,
        out_shape=jax.ShapeDtypeStruct((8, K1 // 2), jnp.int32),
        out_specs=pl.BlockSpec(memory_space=pltpu.VMEM),
        compiler_params=pltpu.CompilerParams(vmem_limit_bytes=4 * 1024 * 1024),
        cost_estimate=cost(4.0),
        name="tables",
    )()


def prep_kernel(table_ref, k1_ref, b1_ref, k2_ref, w1_ref, w2_ref, w2f_ref, flat_ref):
    me = lax.axis_index("aa")

    def lines(ref):
        for n in range(27):
            u, v, w = n // 9, n // 3 % 3, n % 3
            w = w if w == 1 else jnp.where(lax.rem(me, 2) == 0, w, 2 - w)
            flat_ref[3 * n : 3 * n + 3, :] = ref[u, v, w].astype(F32)
        return flat_ref[...].astype(BF)

    tap = table_ref[0:1, :]
    weight = lines(k1_ref)
    row_id = lax.broadcasted_iota(jnp.int32, (81, K1 // 2), 0)
    spread = []
    for uv in range(9):
        pick = jnp.where(row_id == uv * 9 + tap, 1.0, 0.0).astype(BF)
        spread.append(
            lax.dot_general(weight, pick, (((0,), (0,)), ((), ())), preferred_element_type=F32)
        )
    square = (HID, HID)
    on = lax.broadcasted_iota(jnp.int32, square, 0) == lax.broadcasted_iota(jnp.int32, square, 1)
    bias = jnp.sum(jnp.where(on, b1_ref[...], 0.0), axis=1, keepdims=True)
    hi = bias.astype(BF).astype(F32)
    mid = (bias - hi).astype(BF).astype(F32)
    low = bias - hi - mid
    one = jnp.broadcast_to(table_ref[2:3, :], (HID, K1 // 2))
    base = jnp.where(one == 0, hi, jnp.where(one == 1, mid, jnp.where(one == 2, low, 0.0)))
    cell = jnp.broadcast_to(table_ref[1:2, :], (HID, K1 // 2))
    for r in range(AR):
        for j in range(AW):
            for half in range(2):
                block = base if half == r // 3 else jnp.zeros_like(base)
                for u in range(3):
                    for v in range(3):
                        i = r + u - 1
                        if i // 2 == half and 0 <= j + v - 1 < AW:
                            where = i % 2 * AW + j + v - 1
                            block = jnp.where(cell == where, spread[u * 3 + v], block)
                start = (r * AW + j) * HID
                cut = slice(half * (K1 // 2), (half + 1) * (K1 // 2))
                w1_ref[start : start + HID, cut] = block.astype(BF)
    col = lax.broadcasted_iota(jnp.int32, (1, M1), 1)
    chan = lax.bitwise_and(col, HID - 1)
    pick = jnp.where(lax.broadcasted_iota(jnp.int32, (HID, M1), 0) == chan, 1.0, 0.0).astype(BF)
    rows = jnp.dot(lines(k2_ref), pick, preferred_element_type=F32)
    own = lax.broadcasted_iota(jnp.int32, (CELLS, M1), 0)
    own_row = jnp.where(own >= 10, 1, 0) + jnp.where(own >= 20, 1, 0) + jnp.where(own >= 30, 1, 0)
    own_col = own - own_row * AW
    own_cell = lax.bitwise_xor(own_row, me) * AW + own_col
    gap = lax.shift_right_logical(col, 4) - own_cell
    gaps = [
        jnp.where(own_col >= 1, gap, 1000),
        gap,
        jnp.where(own_col <= AW - 2, gap, 1000),
    ]
    for st in range(9):
        block = jnp.zeros((CELLS, M1), F32)
        for u in range(3):
            for v in range(3):
                n = (u * 3 + v) * 9 + st
                block = jnp.where(gaps[v] == (u - 1) * AW + v - 1, rows[n : n + 1, :], block)
        s, t = st // 3, st % 3
        w2f_ref[t * CELLS : (t + 1) * CELLS, s * M1 : (s + 1) * M1] = block
    w2_ref[...] = w2f_ref[...].astype(BF)


def prep(k1, b1, k2):
    vm = pl.BlockSpec(memory_space=pltpu.VMEM)
    return pl.pallas_call(
        prep_kernel,
        out_shape=(
            jax.ShapeDtypeStruct((M1, K1), BF),
            jax.ShapeDtypeStruct((M2, 3 * M1), BF),
        ),
        in_specs=[vm] * 4,
        out_specs=(vm, vm),
        scratch_shapes=[pltpu.VMEM((M2, 3 * M1), F32), pltpu.VMEM((81, HID), F32)],
        compiler_params=pltpu.CompilerParams(vmem_limit_bytes=VMEM_LIMIT),
        cost_estimate=cost(2.0),
        name="prep",
    )(tables(), k1, b1, k2)


def correlation(feats, block):
    product = lax.dot_general(
        feats, block, (((1,), (1,)), ((), ())), preferred_element_type=F32
    )
    value = (product * C ** (-0.5)).astype(BF).astype(F32)
    row = lax.broadcasted_iota(jnp.int32, value.shape, 0)
    filler = (row >= PAD - 4) | ((row >= PAIR - 4) & (row < PAIR))
    return jnp.where(filler, 1.0, value)


def target_row(target_ref, n):
    return target_ref[jnp.where(lax.rem(lax.axis_index("aa"), 2) == 0, n, BR - 1 - n)]


def edge_kernel(s0, s1, s3, s2, target_ref, w1_ref, feats_ref, edge_ref, stage):
    me = lax.axis_index("aa")
    given = [ref[0].astype(F32) for ref in (s0, s1, s2, s3)]
    stage[...] = jnp.zeros_like(stage)
    for n in range(AR):
        pick = given[n ^ 3]
        for k in range(3):
            pick = jnp.where(me == k, given[n ^ k], pick)
        start = n // 2 * PAIR + n % 2 * AW
        stage[start : start + AW, :] = pick
    feats = stage[...].astype(BF)
    feats_ref[...] = feats
    for n in range(2):
        value = correlation(feats, target_row(target_ref, n))
        edge_ref[:, n * BW : (n + 1) * BW] = value.astype(BF)


def edges(sources, target, w1):
    vm = pl.BlockSpec(memory_space=pltpu.VMEM)
    return pl.pallas_call(
        edge_kernel,
        out_shape=(
            jax.ShapeDtypeStruct((PAD, C), BF),
            jax.ShapeDtypeStruct((PAD, 2 * BW), BF),
        ),
        in_specs=[vm] * 5 + [pl.BlockSpec(memory_space=pl.ANY)],
        out_specs=(vm, vm),
        scratch_shapes=[pltpu.VMEM((PAD, C), F32)],
        compiler_params=pltpu.CompilerParams(vmem_limit_bytes=VMEM_LIMIT),
        cost_estimate=cost(2.0),
        name="edges",
    )(sources[0], sources[1], sources[3], sources[2], target, w1)


def three_shifts(value):
    moved = [shifted(value, t) for t in range(3)]
    fill = jnp.zeros((LINE - 3 * PAIR, BW), F32)
    return jnp.concatenate(
        [
            piece
            for n in range(2)
            for piece in (*(m[n * PAIR : (n + 1) * PAIR] for m in moved), fill)
        ],
        axis=0,
    ).astype(BF)


def hidden_row(w1_ref, parts, out_ref, start, drop=None):
    low = jnp.concatenate([part[0:LINE] for part in parts], axis=0)
    high = jnp.concatenate([part[LINE : 2 * LINE] for part in parts], axis=0)
    both = jnp.concatenate([low, jnp.zeros((GAP, BW), BF), high], axis=0)
    for first, rows, begin, x in (
        (0, ROW, 0, low),
        (ROW, 2 * ROW, 0, both),
        (3 * ROW, ROW, HALF + GAP, high),
    ):
        w1 = w1_ref[first : first + rows, begin : begin + x.shape[0]]
        value = jnp.maximum(jnp.dot(w1, x, preferred_element_type=F32), 0.0)
        if drop is not None:
            value = jnp.where(drop, 0.0, value)
        out_ref[start + first : start + first + rows, :] = value.astype(BF)


def sums_of(w2_ref, hidden_ref, s, first, count):
    return jnp.dot(
        w2_ref[:, s * M1 : (s + count) * M1],
        hidden_ref[first * M1 : (first + count) * M1, :],
        preferred_element_type=F32,
    )


def logit_row(sums, b2):
    return (
        sums[CELLS : 2 * CELLS, :]
        + shifted(sums[0:CELLS, :], 0)
        + shifted(sums[2 * CELLS : 3 * CELLS, :], 2)
        + b2
    )


def emit_row(logits, out_ref, n, best):
    mine = logits[0 : 2 * AW, :]
    out_ref[n, 0 : 2 * AW, :] = softplus(mine)
    top = jnp.max(logits, axis=0, keepdims=True)
    out_ref[n, 2 * AW : 2 * AW + 1, :] = softplus(top)
    return mine if best is None else jnp.maximum(best, mine)


def inner_kernel(
    feats_ref, target_ref, edge_ref, w1_ref, w2_ref, b2_ref,
    ready_ref, best_ref, sums_ref, near_ref, x, hidden,
):
    feats = feats_ref[...]
    for n in range(2):
        near_ref[n] = three_shifts(edge_ref[:, n * BW : (n + 1) * BW].astype(F32))
    for n in range(2, OWN + 2):
        x[n - 2] = three_shifts(correlation(feats, target_row(target_ref, n)))
    rows = [near_ref[0], near_ref[1], *(x[n] for n in range(OWN))]
    best = None
    for h in range(OWN):
        hidden_row(w1_ref, rows[h : h + 3], hidden, h * M1)
        if h >= 2:
            logits = logit_row(sums_of(w2_ref, hidden, 0, h - 2, 3), b2_ref[0])
            best = emit_row(logits, ready_ref, h - 2, best)
    best_ref[...] = best
    sums_ref[0] = sums_of(w2_ref, hidden, 2, 0, 1)
    sums_ref[1] = sums_of(w2_ref, hidden, 1, 0, 2)


def inner(feats, target, edge, w1, w2, b2):
    vm = pl.BlockSpec(memory_space=pltpu.VMEM)
    return pl.pallas_call(
        inner_kernel,
        out_shape=(
            jax.ShapeDtypeStruct((2, PAIR, BW), F32),
            jax.ShapeDtypeStruct((2 * AW, BW), F32),
            jax.ShapeDtypeStruct((2, M2, BW), F32),
            jax.ShapeDtypeStruct((2, 2 * LINE, BW), BF),
        ),
        in_specs=[vm] * 5 + [pl.BlockSpec(memory_space=pltpu.SMEM)],
        out_specs=(vm,) * 4,
        scratch_shapes=[
            pltpu.VMEM((OWN, 2 * LINE, BW), BF),
            pltpu.VMEM((OWN * M1, BW), BF),
        ],
        compiler_params=pltpu.CompilerParams(vmem_limit_bytes=VMEM_LIMIT),
        cost_estimate=cost(8.0),
        name="inner",
    )(feats, target, edge, w1, w2, b2)


def outer_kernel(
    blocks, near_ref, halo_ref, w1_ref, w2_ref, b2_ref, sums_ref, best_ref, inner_ref,
    out_ref, mx_ref, hidden,
):
    core = lax.rem(lax.axis_index("aa"), 2)
    outside = lax.axis_index("ba") == jnp.where(core == 0, 0, blocks - 1)
    rows = [
        three_shifts(jnp.where(outside, 0.0, halo_ref[:, n * BW : (n + 1) * BW].astype(F32)))
        for n in (1, 0)
    ] + [near_ref[0], near_ref[1]]
    hidden_row(w1_ref, rows[0:3], hidden, 0, outside)
    hidden_row(w1_ref, rows[1:4], hidden, M1)
    best = best_ref[...]
    for n in range(2):
        sums = sums_ref[n] + sums_of(w2_ref, hidden, 0, n, 2 - n)
        best = emit_row(logit_row(sums, b2_ref[0]), out_ref, n, best)
    out_ref[2:OWN] = inner_ref[...]
    top = jnp.max(best, axis=1, keepdims=True)
    row_id = lax.broadcasted_iota(jnp.int32, (2 * AW, 128), 0)
    lane = lax.broadcasted_iota(jnp.int32, (2 * AW, 128), 1)
    lines = [
        jnp.sum(jnp.where(row_id - n * AW == lane, top, 0.0), axis=0, keepdims=True)
        for n in range(2)
    ]
    lane = lane[0:1]
    lines = [jnp.where(lane < AW, line, 0.0) for line in lines]
    for n in range(2):
        line = jnp.where(core == n, lines[0], lines[1])
        mx_ref[n * blocks : (n + 1) * blocks, :] = jnp.broadcast_to(line, (blocks, 128))


def outer(blocks, near, halo, w1, w2, b2, sums, best, ready):
    vm = pl.BlockSpec(memory_space=pltpu.VMEM)
    return pl.pallas_call(
        functools.partial(outer_kernel, blocks),
        out_shape=(
            jax.ShapeDtypeStruct((OWN, PAIR, BW), F32),
            jax.ShapeDtypeStruct((2 * blocks, 128), F32),
        ),
        in_specs=[vm] * 4 + [pl.BlockSpec(memory_space=pltpu.SMEM)] + [vm] * 3,
        out_specs=(vm, vm),
        scratch_shapes=[pltpu.VMEM((2 * M1, BW), BF)],
        compiler_params=pltpu.CompilerParams(vmem_limit_bytes=VMEM_LIMIT),
        cost_estimate=cost(4.0),
        name="outer",
    )(near, halo, w1, w2, b2, sums, best, ready)


def final_kernel(own_ref, other_ref, mx_ref, out_ref):
    upper = lax.rem(lax.axis_index("aa"), 2) == 0
    top = softplus(jnp.max(mx_ref[...], axis=0, keepdims=True))
    row_id = lax.broadcasted_iota(jnp.int32, (AW, 128), 0)
    lane = lax.broadcasted_iota(jnp.int32, (AW, 128), 1)
    cell = jnp.sum(jnp.where(row_id == lane, top, 0.0), axis=1, keepdims=True) + EPS
    for p in range(BR):
        n = min(p, BR - 1 - p)
        here = upper if p < OWN else jnp.logical_not(upper)
        s = jnp.where(here, own_ref[n, 0:AW, :], other_ref[n, AW : 2 * AW, :])
        best = 2 * AW, 2 * AW + 1
        best = jnp.where(
            here, own_ref[n, best[0] : best[1], :], other_ref[n, best[0] : best[1], :]
        )
        value = s * (s / (best + EPS)) * (s / cell)
        for j in range(AW):
            out_ref[0, j, p : p + 1, :] = value[j : j + 1, :]


def finish(own, other, mx):
    vm = pl.BlockSpec(memory_space=pltpu.VMEM)
    return pl.pallas_call(
        final_kernel,
        out_shape=jax.ShapeDtypeStruct((1, AW, BR, BW), F32),
        in_specs=[vm] * 3,
        out_specs=vm,
        compiler_params=pltpu.CompilerParams(vmem_limit_bytes=4 * 1024 * 1024),
        name="finish",
    )(own, other, mx)


def neighbour(a, i, blocks):
    j = i + 2 * (a % 2) - 1
    return (a ^ 1) * blocks + j if 0 <= j < blocks else (a ^ 2) * blocks + i


def per_device(source, target, first_kernel, first_bias, second_kernel, second_bias):
    blocks = lax.axis_size("ba")
    size = lax.axis_size("aa")
    twin = [(i, i ^ 1) for i in range(size)]
    beside = lax.ppermute(source, "aa", twin)
    far = lax.ppermute(source, "aa", [(i, i ^ 3) for i in range(size)])
    w1, w2 = prep(
        jnp.transpose(first_kernel[:, 0], (1, 2, 3, 4, 0)),
        first_bias[None, :],
        jnp.transpose(second_kernel[0], (1, 2, 3, 4, 0)),
    )
    far, w1, w2 = lax.optimization_barrier((far, w1, w2))
    sources = [source, beside, lax.ppermute(far, "aa", twin), far]
    feats, edge = edges(sources, target, w1)
    halo = lax.ppermute(
        edge,
        ("aa", "ba"),
        [
            (a * blocks + i, neighbour(a, i, blocks))
            for a in range(size)
            for i in range(blocks)
        ],
    )
    ready, best, sums, near = inner(feats, target, edge, w1, w2, second_bias)
    own, mx = outer(blocks, near, halo, w1, w2, second_bias, sums, best, ready)
    other = lax.ppermute(own, "aa", [(i, i ^ 1) for i in range(size)])
    mx = lax.all_to_all(
        mx,
        ("aa", "ba"),
        0,
        0,
        tiled=True,
        axis_index_groups=[
            [(a + c) * blocks + i for c in range(2) for i in range(blocks)]
            for a in range(0, size, 2)
        ],
    )
    return finish(own, other, mx)


def solution(mesh):
    return jax.shard_map(
        per_device,
        mesh=mesh,
        in_specs=(P("aa", None, None), P("ba", None, None), P(), P(), P(), P()),
        out_specs=P("aa", None, "ba", None),
        check_vma=False,
    )
```

```python
import functools

import jax
import jax.numpy as jnp
from jax import lax
from jax.experimental import pallas as pl
from jax.experimental.pallas import tpu as pltpu
from jax.sharding import PartitionSpec as P

C = 1024
HID = 16
AW = 10
AR = 4
CELLS = AR * AW
PAIR = 24
PAD = 2 * PAIR
BW = 512
BR = 8
LINE = 80
HALF = 3 * LINE
GAP = 16
K1 = 2 * (HALF + GAP)
ROW = AW * HID
OWN = BR // 2
M1 = AR * ROW
M2 = 3 * CELLS
EPS = 1e-5
BF = jnp.bfloat16
F32 = jnp.float32
VMEM_LIMIT = 20 * 1024 * 1024


def cost(us):
    return pl.CostEstimate(flops=int(us * 1e9), bytes_accessed=int(us * 3e6), transcendentals=0)


def softplus(v):
    return jnp.maximum(v, 0.0) + jnp.log1p(jnp.exp(-jnp.abs(v)))


def shifted(x, t):
    if t == 1:
        return x
    lane = lax.broadcasted_iota(jnp.int32, x.shape, 1)
    if t == 0:
        return jnp.where(lane == 0, 0.0, pltpu.roll(x, 1, 1))
    return jnp.where(lane == BW - 1, 0.0, pltpu.roll(x, BW - 1, 1))


def table_kernel(out_ref):
    col = lax.broadcasted_iota(jnp.int32, (8, K1 // 2), 1)
    s = lax.shift_right_logical(col * 820, 16)
    rest = col - s * LINE
    t = lax.shift_right_logical(rest * 2731, 16)
    place = rest - t * PAIR
    real = (s < 3) & (t < 3)
    tap = s * 3 + t
    cell = jnp.where(real & (place < 2 * AW), place, -1000)
    one = jnp.where(real & (tap == 4) & (place >= 2 * AW), place - 2 * AW, -1000)
    row = lax.broadcasted_iota(jnp.int32, (8, K1 // 2), 0)
    out_ref[...] = jnp.where(row == 0, tap, jnp.where(row == 1, cell, one))


def tables():
    return pl.pallas_call(
        table_kernel,
        out_shape=jax.ShapeDtypeStruct((8, K1 // 2), jnp.int32),
        out_specs=pl.BlockSpec(memory_space=pltpu.VMEM),
        compiler_params=pltpu.CompilerParams(vmem_limit_bytes=4 * 1024 * 1024),
        cost_estimate=cost(4.0),
        name="tables",
    )()


def prep_kernel(table_ref, k1_ref, b1_ref, k2_ref, w1_ref, w2_ref, w2f_ref, flat_ref):
    me = lax.axis_index("aa")

    def lines(ref):
        for n in range(27):
            u, v, w = n // 9, n // 3 % 3, n % 3
            w = w if w == 1 else jnp.where(lax.rem(me, 2) == 0, w, 2 - w)
            flat_ref[3 * n : 3 * n + 3, :] = ref[u, v, w].astype(F32)
        return flat_ref[...].astype(BF)

    tap = table_ref[0:1, :]
    weight = lines(k1_ref)
    row_id = lax.broadcasted_iota(jnp.int32, (81, K1 // 2), 0)
    spread = []
    for uv in range(9):
        pick = jnp.where(row_id == uv * 9 + tap, 1.0, 0.0).astype(BF)
        spread.append(
            lax.dot_general(weight, pick, (((0,), (0,)), ((), ())), preferred_element_type=F32)
        )
    square = (HID, HID)
    on = lax.broadcasted_iota(jnp.int32, square, 0) == lax.broadcasted_iota(jnp.int32, square, 1)
    bias = jnp.sum(jnp.where(on, b1_ref[...], 0.0), axis=1, keepdims=True)
    hi = bias.astype(BF).astype(F32)
    mid = (bias - hi).astype(BF).astype(F32)
    low = bias - hi - mid
    one = jnp.broadcast_to(table_ref[2:3, :], (HID, K1 // 2))
    base = jnp.where(one == 0, hi, jnp.where(one == 1, mid, jnp.where(one == 2, low, 0.0)))
    cell = jnp.broadcast_to(table_ref[1:2, :], (HID, K1 // 2))
    for r in range(AR):
        for j in range(AW):
            for half in range(2):
                block = base if half == r // 3 else jnp.zeros_like(base)
                for u in range(3):
                    for v in range(3):
                        i = r + u - 1
                        if i // 2 == half and 0 <= j + v - 1 < AW:
                            where = i % 2 * AW + j + v - 1
                            block = jnp.where(cell == where, spread[u * 3 + v], block)
                start = (r * AW + j) * HID
                cut = slice(half * (K1 // 2), (half + 1) * (K1 // 2))
                w1_ref[start : start + HID, cut] = block.astype(BF)
    col = lax.broadcasted_iota(jnp.int32, (1, M1), 1)
    chan = lax.bitwise_and(col, HID - 1)
    pick = jnp.where(lax.broadcasted_iota(jnp.int32, (HID, M1), 0) == chan, 1.0, 0.0).astype(BF)
    rows = jnp.dot(lines(k2_ref), pick, preferred_element_type=F32)
    own = lax.broadcasted_iota(jnp.int32, (CELLS, M1), 0)
    own_row = jnp.where(own >= 10, 1, 0) + jnp.where(own >= 20, 1, 0) + jnp.where(own >= 30, 1, 0)
    own_col = own - own_row * AW
    own_cell = lax.bitwise_xor(own_row, me) * AW + own_col
    gap = lax.shift_right_logical(col, 4) - own_cell
    gaps = [
        jnp.where(own_col >= 1, gap, 1000),
        gap,
        jnp.where(own_col <= AW - 2, gap, 1000),
    ]
    for st in range(9):
        block = jnp.zeros((CELLS, M1), F32)
        for u in range(3):
            for v in range(3):
                n = (u * 3 + v) * 9 + st
                block = jnp.where(gaps[v] == (u - 1) * AW + v - 1, rows[n : n + 1, :], block)
        s, t = st // 3, st % 3
        w2f_ref[t * CELLS : (t + 1) * CELLS, s * M1 : (s + 1) * M1] = block
    w2_ref[...] = w2f_ref[...].astype(BF)


def prep(k1, b1, k2):
    vm = pl.BlockSpec(memory_space=pltpu.VMEM)
    return pl.pallas_call(
        prep_kernel,
        out_shape=(
            jax.ShapeDtypeStruct((M1, K1), BF),
            jax.ShapeDtypeStruct((M2, 3 * M1), BF),
        ),
        in_specs=[vm] * 4,
        out_specs=(vm, vm),
        scratch_shapes=[pltpu.VMEM((M2, 3 * M1), F32), pltpu.VMEM((81, HID), F32)],
        compiler_params=pltpu.CompilerParams(vmem_limit_bytes=VMEM_LIMIT),
        cost_estimate=cost(2.0),
        name="prep",
    )(tables(), k1, b1, k2)


def correlation(feats, block):
    product = lax.dot_general(
        feats, block, (((1,), (1,)), ((), ())), preferred_element_type=F32
    )
    value = (product * C ** (-0.5)).astype(BF).astype(F32)
    row = lax.broadcasted_iota(jnp.int32, value.shape, 0)
    filler = (row >= PAD - 4) | ((row >= PAIR - 4) & (row < PAIR))
    return jnp.where(filler, 1.0, value)


def target_row(target_ref, n):
    return target_ref[jnp.where(lax.rem(lax.axis_index("aa"), 2) == 0, n, BR - 1 - n)]


def edge_kernel(s0, s1, s3, s2, target_ref, w1_ref, feats_ref, edge_ref, stage):
    me = lax.axis_index("aa")
    given = [ref[0].astype(F32) for ref in (s0, s1, s2, s3)]
    stage[...] = jnp.zeros_like(stage)
    for n in range(AR):
        pick = given[n ^ 3]
        for k in range(3):
            pick = jnp.where(me == k, given[n ^ k], pick)
        start = n // 2 * PAIR + n % 2 * AW
        stage[start : start + AW, :] = pick
    feats = stage[...].astype(BF)
    feats_ref[...] = feats
    for n in range(2):
        value = correlation(feats, target_row(target_ref, n))
        edge_ref[:, n * BW : (n + 1) * BW] = value.astype(BF)


def edges(sources, target, w1):
    vm = pl.BlockSpec(memory_space=pltpu.VMEM)
    return pl.pallas_call(
        edge_kernel,
        out_shape=(
            jax.ShapeDtypeStruct((PAD, C), BF),
            jax.ShapeDtypeStruct((PAD, 2 * BW), BF),
        ),
        in_specs=[vm] * 5 + [pl.BlockSpec(memory_space=pl.ANY)],
        out_specs=(vm, vm),
        scratch_shapes=[pltpu.VMEM((PAD, C), F32)],
        compiler_params=pltpu.CompilerParams(vmem_limit_bytes=VMEM_LIMIT),
        cost_estimate=cost(2.0),
        name="edges",
    )(sources[0], sources[1], sources[3], sources[2], target, w1)


def three_shifts(value):
    moved = [shifted(value, t) for t in range(3)]
    fill = jnp.zeros((LINE - 3 * PAIR, BW), F32)
    return jnp.concatenate(
        [
            piece
            for n in range(2)
            for piece in (*(m[n * PAIR : (n + 1) * PAIR] for m in moved), fill)
        ],
        axis=0,
    ).astype(BF)


def hidden_row(w1_ref, parts, out_ref, start, drop=None):
    low = jnp.concatenate([part[0:LINE] for part in parts], axis=0)
    high = jnp.concatenate([part[LINE : 2 * LINE] for part in parts], axis=0)
    both = jnp.concatenate([low, jnp.zeros((GAP, BW), BF), high], axis=0)
    for first, rows, begin, x in (
        (0, ROW, 0, low),
        (ROW, 2 * ROW, 0, both),
        (3 * ROW, ROW, HALF + GAP, high),
    ):
        w1 = w1_ref[first : first + rows, begin : begin + x.shape[0]]
        value = jnp.maximum(jnp.dot(w1, x, preferred_element_type=F32), 0.0)
        if drop is not None:
            value = jnp.where(drop, 0.0, value)
        out_ref[start + first : start + first + rows, :] = value.astype(BF)


def sums_of(w2_ref, hidden_ref, s, first, count):
    return jnp.dot(
        w2_ref[:, s * M1 : (s + count) * M1],
        hidden_ref[first * M1 : (first + count) * M1, :],
        preferred_element_type=F32,
    )


def logit_row(sums, b2):
    return (
        sums[CELLS : 2 * CELLS, :]
        + shifted(sums[0:CELLS, :], 0)
        + shifted(sums[2 * CELLS : 3 * CELLS, :], 2)
        + b2
    )


def emit_row(logits, out_ref, n, best):
    mine = logits[0 : 2 * AW, :]
    out_ref[n, 0 : 2 * AW, :] = softplus(mine)
    top = jnp.max(logits, axis=0, keepdims=True)
    out_ref[n, 2 * AW : 2 * AW + 1, :] = softplus(top)
    return mine if best is None else jnp.maximum(best, mine)


def inner_kernel(
    feats_ref, target_ref, edge_ref, w1_ref, w2_ref, b2_ref,
    ready_ref, best_ref, sums_ref, near_ref, x, hidden,
):
    feats = feats_ref[...]
    for n in range(2):
        near_ref[n] = three_shifts(edge_ref[:, n * BW : (n + 1) * BW].astype(F32))
    for n in range(2, OWN + 2):
        x[n - 2] = three_shifts(correlation(feats, target_row(target_ref, n)))
    rows = [near_ref[0], near_ref[1], *(x[n] for n in range(OWN))]
    best = None
    for h in range(OWN):
        hidden_row(w1_ref, rows[h : h + 3], hidden, h * M1)
        if h >= 2:
            logits = logit_row(sums_of(w2_ref, hidden, 0, h - 2, 3), b2_ref[0])
            best = emit_row(logits, ready_ref, h - 2, best)
    best_ref[...] = best
    sums_ref[0] = sums_of(w2_ref, hidden, 2, 0, 1)
    sums_ref[1] = sums_of(w2_ref, hidden, 1, 0, 2)


def inner(feats, target, edge, w1, w2, b2):
    vm = pl.BlockSpec(memory_space=pltpu.VMEM)
    return pl.pallas_call(
        inner_kernel,
        out_shape=(
            jax.ShapeDtypeStruct((2, PAIR, BW), F32),
            jax.ShapeDtypeStruct((2 * AW, BW), F32),
            jax.ShapeDtypeStruct((2, M2, BW), F32),
            jax.ShapeDtypeStruct((2, 2 * LINE, BW), BF),
        ),
        in_specs=[vm] * 5 + [pl.BlockSpec(memory_space=pltpu.SMEM)],
        out_specs=(vm,) * 4,
        scratch_shapes=[
            pltpu.VMEM((OWN, 2 * LINE, BW), BF),
            pltpu.VMEM((OWN * M1, BW), BF),
        ],
        compiler_params=pltpu.CompilerParams(vmem_limit_bytes=VMEM_LIMIT),
        cost_estimate=cost(8.0),
        name="inner",
    )(feats, target, edge, w1, w2, b2)


def outer_kernel(
    blocks, near_ref, halo_ref, w1_ref, w2_ref, b2_ref, sums_ref, best_ref, inner_ref,
    out_ref, mx_ref, hidden,
):
    core = lax.rem(lax.axis_index("aa"), 2)
    outside = lax.axis_index("ba") == jnp.where(core == 0, 0, blocks - 1)
    rows = [
        three_shifts(jnp.where(outside, 0.0, halo_ref[:, n * BW : (n + 1) * BW].astype(F32)))
        for n in (1, 0)
    ] + [near_ref[0], near_ref[1]]
    hidden_row(w1_ref, rows[0:3], hidden, 0, outside)
    hidden_row(w1_ref, rows[1:4], hidden, M1)
    best = best_ref[...]
    for n in range(2):
        sums = sums_ref[n] + sums_of(w2_ref, hidden, 0, n, 2 - n)
        best = emit_row(logit_row(sums, b2_ref[0]), out_ref, n, best)
    out_ref[2:OWN] = inner_ref[...]
    top = jnp.max(best, axis=1, keepdims=True)
    row_id = lax.broadcasted_iota(jnp.int32, (2 * AW, 128), 0)
    lane = lax.broadcasted_iota(jnp.int32, (2 * AW, 128), 1)
    lines = [
        jnp.sum(jnp.where(row_id - n * AW == lane, top, 0.0), axis=0, keepdims=True)
        for n in range(2)
    ]
    lane = lane[0:1]
    lines = [jnp.where(lane < AW, line, 0.0) for line in lines]
    for n in range(2):
        line = jnp.where(core == n, lines[0], lines[1])
        mx_ref[n * blocks : (n + 1) * blocks, :] = jnp.broadcast_to(line, (blocks, 128))


def outer(blocks, near, halo, w1, w2, b2, sums, best, ready):
    vm = pl.BlockSpec(memory_space=pltpu.VMEM)
    return pl.pallas_call(
        functools.partial(outer_kernel, blocks),
        out_shape=(
            jax.ShapeDtypeStruct((OWN, PAIR, BW), F32),
            jax.ShapeDtypeStruct((2 * blocks, 128), F32),
        ),
        in_specs=[vm] * 4 + [pl.BlockSpec(memory_space=pltpu.SMEM)] + [vm] * 3,
        out_specs=(vm, vm),
        scratch_shapes=[pltpu.VMEM((2 * M1, BW), BF)],
        compiler_params=pltpu.CompilerParams(vmem_limit_bytes=VMEM_LIMIT),
        cost_estimate=cost(4.0),
        name="outer",
    )(near, halo, w1, w2, b2, sums, best, ready)


def final_kernel(own_ref, other_ref, mx_ref, out_ref):
    upper = lax.rem(lax.axis_index("aa"), 2) == 0
    top = softplus(jnp.max(mx_ref[...], axis=0, keepdims=True))
    row_id = lax.broadcasted_iota(jnp.int32, (AW, 128), 0)
    lane = lax.broadcasted_iota(jnp.int32, (AW, 128), 1)
    cell = jnp.sum(jnp.where(row_id == lane, top, 0.0), axis=1, keepdims=True) + EPS
    share = 1.0 / cell
    for p in range(BR):
        n = min(p, BR - 1 - p)
        here = upper if p < OWN else jnp.logical_not(upper)
        s = jnp.where(here, own_ref[n, 0:AW, :], other_ref[n, AW : 2 * AW, :])
        best = 2 * AW, 2 * AW + 1
        best = jnp.where(
            here, own_ref[n, best[0] : best[1], :], other_ref[n, best[0] : best[1], :]
        )
        value = s * (s * (1.0 / (best + EPS))) * (s * share)
        for j in range(AW):
            out_ref[0, j, p : p + 1, :] = value[j : j + 1, :]


def finish(own, other, mx):
    vm = pl.BlockSpec(memory_space=pltpu.VMEM)
    return pl.pallas_call(
        final_kernel,
        out_shape=jax.ShapeDtypeStruct((1, AW, BR, BW), F32),
        in_specs=[vm] * 3,
        out_specs=vm,
        compiler_params=pltpu.CompilerParams(vmem_limit_bytes=4 * 1024 * 1024),
        name="finish",
    )(own, other, mx)


def neighbour(a, i, blocks):
    j = i + 2 * (a % 2) - 1
    return (a ^ 1) * blocks + j if 0 <= j < blocks else (a ^ 2) * blocks + i


def per_device(source, target, first_kernel, first_bias, second_kernel, second_bias):
    blocks = lax.axis_size("ba")
    size = lax.axis_size("aa")
    twin = [(i, i ^ 1) for i in range(size)]
    beside = lax.ppermute(source, "aa", twin)
    far = lax.ppermute(source, "aa", [(i, i ^ 3) for i in range(size)])
    w1, w2 = prep(
        jnp.transpose(first_kernel[:, 0], (1, 2, 3, 4, 0)),
        first_bias[None, :],
        jnp.transpose(second_kernel[0], (1, 2, 3, 4, 0)),
    )
    far, w1, w2 = lax.optimization_barrier((far, w1, w2))
    sources = [source, beside, lax.ppermute(far, "aa", twin), far]
    feats, edge = edges(sources, target, w1)
    halo = lax.ppermute(
        edge,
        ("aa", "ba"),
        [
            (a * blocks + i, neighbour(a, i, blocks))
            for a in range(size)
            for i in range(blocks)
        ],
    )
    ready, best, sums, near = inner(feats, target, edge, w1, w2, second_bias)
    own, mx = outer(blocks, near, halo, w1, w2, second_bias, sums, best, ready)
    other = lax.ppermute(own, "aa", [(i, i ^ 1) for i in range(size)])
    mx = lax.all_to_all(
        mx,
        ("aa", "ba"),
        0,
        0,
        tiled=True,
        axis_index_groups=[
            [(a + c) * blocks + i for c in range(2) for i in reversed(range(blocks))]
            for a in range(0, size, 2)
        ],
    )
    return finish(own, other, mx)


def solution(mesh):
    return jax.shard_map(
        per_device,
        mesh=mesh,
        in_specs=(P("aa", None, None), P("ba", None, None), P(), P(), P(), P()),
        out_specs=P("aa", None, "ba", None),
        check_vma=False,
    )
```
